256 devices in a mesh: sub: 64 (over z, x, core), blk: 4 (over y).
Axes of the slice: x: 4, y: 4, z: 8, core: 2. Of those that a mesh axis runs over, the one named last changes fastest.
Arguments:
- a_tiles: bfloat16 [6144, 12, 128, 128], P(('sub', 'blk'))
- modes: bfloat16 [6144, 16, 128], P(('sub', 'blk')), may hold values from -6 to 6
- col_tiles: int32 [6144, 12], P(('sub', 'blk')), may hold values from 0 to 225, as said below
- fetch_list: int32 [256, 130], P(('sub', 'blk')), may hold values from 0 to 6143, as said below
Outputs:
- prolong: bfloat16 [6144, 12, 16, 128], P(('sub', 'blk'))
- coarse_diag: float32 [6144, 256], P('sub')
The draws below stay inside these ranges and needn't reach their ends.
Inputs may be any that keep to these rules, and one draw needn't show every extreme that they name: `col_tiles`: slot 0 of row tile t names t itself (its index within its group); the other slots name other tiles of the same group (values below 96) or 96 + h for entry h of the device's fetch list; every entry of a device's fetch list is named by some slot of that device's rows. `fetch_list`: A device's list is 26 blocks of 5 entries; each block names distinct tiles of one group other than the device's own, different blocks name different groups; tile i of group g has number g * 96 + i.
All inputs are finite; a program needn't handle non-finite values.
Results may differ from the reference program's by a relative error of at most 0.008.
Values may be sent and summed in bfloat16 or wider, within the bound.
A program may use at most 64 MiB of HBM per device.

```python
import jax
import jax.numpy as jnp
from jax import lax

TILE_DEV = 24
SLOTS = 12
TILE_ROWS = 128
MODES = 16
PEERS = 26
PER_PEER = 5
GHOSTS = 130
GROUP = 96
TILES = 6144
N_SUB = 64
N_BLK = 4


def draw_a_tiles(key, part):
    first_key, second_key = jax.random.split(key, 2)
    shape = (TILES, SLOTS, TILE_ROWS, TILE_ROWS)
    offdiag = jax.random.normal(first_key, shape, jnp.float32) * TILE_ROWS ** (-0.5)
    diagonal = jax.random.uniform(second_key, shape, jnp.float32, 1.0, 3.0)
    slot_index = lax.broadcasted_iota(jnp.int32, shape, 1)
    row_index = lax.broadcasted_iota(jnp.int32, shape, 2)
    col_index = lax.broadcasted_iota(jnp.int32, shape, 3)
    values = jnp.where((slot_index == 0) & (row_index == col_index), diagonal, offdiag)
    return values.astype(jnp.bfloat16)


def draw_col_tiles(key, part):

    def per_device(device):
        first_key, second_key = jax.random.split(jax.random.fold_in(key, device))
        count = TILE_DEV * (SLOTS - 1)
        order = jax.random.permutation(first_key, count)
        random_rows = jax.random.randint(second_key, (count,), 0, GROUP - 1)
        itself = device % N_BLK * TILE_DEV + jnp.repeat(jnp.arange(TILE_DEV, dtype=jnp.int32), SLOTS - 1)
        others = random_rows + (random_rows >= itself).astype(jnp.int32)
        filled = jnp.where(order < GHOSTS, GROUP + order, others).reshape(TILE_DEV, SLOTS - 1)
        leading = device % N_BLK * TILE_DEV + jnp.arange(TILE_DEV, dtype=jnp.int32)
        return jnp.concatenate([leading[:, None], filled], axis=1)
    return jax.vmap(per_device)(jnp.arange(N_SUB * N_BLK, dtype=jnp.int32)).reshape(TILES, SLOTS).astype(jnp.int32)


def draw_fetch_list(key, part):

    def per_device(device):
        group_index = device // N_BLK
        first_key, second_key = jax.random.split(jax.random.fold_in(key, device))
        chosen = jax.random.permutation(first_key, N_SUB - 1)[:PEERS]
        groups = chosen + (chosen >= group_index).astype(jnp.int32)
        group_keys = jax.random.split(second_key, PEERS)

        def members(member_key):
            return jax.random.permutation(member_key, GROUP)[:PER_PEER]
        within = jax.vmap(members)(group_keys)
        return (groups[:, None] * GROUP + within).reshape(GHOSTS)
    return jax.vmap(per_device)(jnp.arange(N_SUB * N_BLK, dtype=jnp.int32)).astype(jnp.int32)


def levels(stream_key, extent, cuts, smallest, high):
    loudness, own = 1.0, jax.random.fold_in(stream_key, 6)
    for dim, blocks in cuts:
        heights = jnp.exp(jax.random.uniform(jax.random.fold_in(own, dim), (blocks,), jnp.float32, smallest / len(cuts), high / len(cuts)))
        loudness = loudness * jnp.repeat(heights, extent[dim] // blocks).reshape([-1 if axis == dim else 1 for axis in range(len(extent))])
    return loudness


def centred(own_key, extent, width, bound, cuts=(), kind=jnp.bfloat16):
    level = levels(own_key, extent, cuts, -0.22, 0.18) if cuts else 1.0
    drawn = jax.random.normal(own_key, extent, jnp.float32) * width * level
    return jnp.minimum(jnp.maximum(drawn, -bound), bound).astype(kind)


def setup_inputs(seed: int = 0) -> dict:
    key_list = jax.random.split(jax.random.key(seed), 5)
    return {
        "a_tiles": draw_a_tiles(jax.random.fold_in(key_list[4], 71), 0),
        "modes": centred(key_list[1], (TILES, MODES, TILE_ROWS), 1.0, 6.0, ((0, 256),)),
        "col_tiles": draw_col_tiles(jax.random.fold_in(key_list[4], 71), 0),
        "fetch_list": draw_fetch_list(jax.random.fold_in(key_list[4], 71), 0),
    }


damping = 2.0 / 3.0


def reference(a_tiles, modes, col_tiles, fetch_list):
    def per_device(coarse_sum, device):
        tiles_here = lax.dynamic_slice_in_dim(a_tiles, device * TILE_DEV, TILE_DEV, 0)
        slots_here = lax.dynamic_slice_in_dim(col_tiles, device * TILE_DEV, TILE_DEV, 0)
        modes_here = lax.dynamic_slice_in_dim(modes, device * TILE_DEV, TILE_DEV, 0)
        fetched = lax.dynamic_index_in_dim(fetch_list, device, 0, keepdims=False)
        group_index = device // N_BLK
        remote = fetched[jnp.clip(slots_here - GROUP, 0, GHOSTS - 1)]
        columns = jnp.where(slots_here < GROUP, group_index * GROUP + slots_here, remote).astype(jnp.int32)
        picked = modes[columns]
        product = jnp.einsum("tkrc,tkmc->tkmr", tiles_here.astype(jnp.float32), picked.astype(jnp.float32),
                             precision=lax.Precision.HIGHEST)
        inverse = 1.0 / jnp.diagonal(tiles_here[:, 0], axis1=1, axis2=2).astype(jnp.float32)
        leading = (jnp.arange(SLOTS) == 0).astype(jnp.float32)
        prolong = (leading[None, :, None, None] * modes_here.astype(jnp.float32)[:, None]
                   - damping * inverse[:, None, None, :] * product).astype(jnp.bfloat16)
        partial_value = jnp.einsum("tkmr,tknr->tkmn", prolong.astype(jnp.float32), product,
                             precision=lax.Precision.HIGHEST) / TILE_ROWS
        coarse_sum = coarse_sum.at[columns.reshape(-1)].add(partial_value.reshape(-1, MODES * MODES))
        return coarse_sum, prolong

    start = jnp.zeros((TILES, MODES * MODES), jnp.float32)
    coarse_diag, prolongs = lax.scan(per_device, start, jnp.arange(N_SUB * N_BLK, dtype=jnp.int32))
    return prolongs.reshape(TILES, SLOTS, MODES, TILE_ROWS), coarse_diag
```

```python
import functools

import jax
import jax.numpy as jnp
from jax import lax
from jax.experimental import pallas as pl
from jax.experimental.pallas import tpu as pltpu
from jax.sharding import PartitionSpec as P

MESH = pl.DeviceIdType.MESH
BF = jnp.bfloat16
F32 = jnp.float32
NZ, NX, NC, NY = 8, 4, 2, 4
TILE_DEV = 24
SLOTS = 12
SLOTP = 16
ROWS = 128
MODES = 16
GROUP = 96
GROUPS = NZ * NX * NC
TILES = GROUP * GROUPS
PER_PEER = 5
GHOSTS = 130
GHOSTP = 144
LIST = 256
NQ = 2
XQ = NX // NQ
OUT_ROWS = GROUP + GROUPS * 8
DAMPING = 2.0 / 3.0


def dev(z, x, c, y):
    return ((z * NX + x) * NC + c, y)


def rcopy(src, dst, send, recv, device):
    return pltpu.make_async_remote_copy(
        src_ref=src, dst_ref=dst, send_sem=send, recv_sem=recv, device_id=device, device_id_type=MESH
    )


def dot_t(a, b):
    return lax.dot_general(a, b, (((1,), (1,)), ((), ())), preferred_element_type=F32)


def body(
    modes, fetch_v, fetch_s, col_s, col_v, a_hbm, prolong, coarse,
    a_v, mf, s1, blocks, rows_f, lists_v, lists_s, stage, msg, got, got_f, table,
    pv, qv, flat, seg, req, idx1, idx2, target, out, in1, in2, ysum,
    a_sem, scat_s, scat_r, list_s, list_r, own_sem, all_s, all_r, ring_s, ring_r, sib_s, sib_r,
    ex_s, ex_r, id1_s, id1_r, id2_s, id2_r, c1_s, c1_r, c2_s, c2_r, y_s, y_r, p_sem,
):
    s = lax.axis_index("sub")
    y = lax.axis_index("blk")
    z, x, c = s // (NX * NC), lax.rem(s // NC, NX), lax.rem(s, NC)
    me = x * NY + y
    xc = x * NC + c
    right, left = dev(lax.rem(z + 1, NZ), x, c, y), dev(lax.rem(z + NZ - 1, NZ), x, c, y)
    sibling = dev(z, x, 1 - c, y)

    def plane(p):
        tx, ty = lax.rem(x + p // NY, NX), lax.rem(y + p % NY, NY)
        return tx * NY + ty, dev(z, tx, c, ty)

    def along_z(d):
        tz = lax.rem(z + d, NZ)
        return tz, dev(tz, x, c, y)

    def across(d):
        t = lax.rem(xc + d, NX * NC)
        return t, (z * NX * NC + t, y)

    def along_y(d):
        return dev(z, x, c, lax.rem(y + d, NY))

    for t in range(TILE_DEV):
        pltpu.make_async_copy(a_hbm.at[t], a_v.at[t], a_sem.at[t]).start()

    barrier = pltpu.get_barrier_semaphore()
    partners = [plane(p)[1] for p in range(1, NX * NY)]
    partners += [along_z(d)[1] for d in range(1, NZ)]
    partners += [dev(z, lax.rem(x + d, NX), 1 - c, y) for d in range(NX)]
    for partner in partners:
        pl.semaphore_signal(barrier, inc=1, device_id=partner, device_id_type=MESH)

    mf[...] = modes[...].astype(F32).reshape(TILE_DEV * MODES, ROWS)
    for m in range(MODES):
        s1[m] = mf[pl.ds(m, TILE_DEV, stride=MODES), :].astype(BF)

    lane = lax.broadcasted_iota(jnp.int32, (8, 128), 1)
    sub8 = lax.broadcasted_iota(jnp.int32, (8, 128), 0)
    request = jnp.full((8, 128), -1, jnp.int32)
    slots = col_v[...]
    colvec = slots
    for h in range(GHOSTS):
        tile = fetch_s[0, h]
        group = tile // GROUP
        request = jnp.where(
            (lane == group) & (sub8 == h % PER_PEER), tile - group * GROUP, request
        )
        slots = jnp.where(colvec == GROUP + h, GROUP + group * 8 + h % PER_PEER, slots)
    req[...] = request

    pl.semaphore_wait(barrier, len(partners))

    pltpu.make_async_copy(s1.at[me], blocks.at[z, c, x, y], scat_r.at[x]).start()
    for p in range(1, NX * NY):
        t, device = plane(p)
        rcopy(s1.at[t], blocks.at[z, c, x, y], scat_s.at[0], scat_r.at[x], device).start()
    pltpu.make_async_copy(fetch_v, lists_v.at[me], own_sem.at[0]).start()
    for p in range(1, NX * NY):
        rcopy(fetch_v, lists_v.at[me], list_s.at[0], list_r.at[0], plane(p)[1]).start()
    for d in range(1, NZ):
        rcopy(req, idx1.at[z], id1_s.at[0], id1_r.at[0], along_z(d)[1]).start()
    mine = table.at[pl.ds(y * TILE_DEV, TILE_DEV)]
    pltpu.make_async_copy(modes, mine, own_sem.at[1]).start()
    for d in range(1, NY):
        rcopy(modes, mine, all_s.at[0], all_r.at[0], along_y(d)).start()
    idx1[z] = request

    def piece(k, core, q):
        return blocks.at[k, core, pl.ds(q * XQ, XQ)]

    def ring(way, step, q, k):
        part = piece(k, c, q)
        device = right if way == 0 else left
        rcopy(part, part, ring_s.at[0], ring_r.at[way, step, q], device).start()

    def pass_on(way, step, q, k):
        part = piece(k, c, q)
        rcopy(part, part, sib_s.at[0], sib_r.at[way, step, q], sibling).start()

    def widen(k, core, q):
        @pl.loop(0, XQ * NY)
        def _(i):
            xs, ys = q * XQ + i // NY, lax.rem(i, NY)
            base = ((k * NX + xs) * NC + core) * GROUP + ys * TILE_DEV
            rows_f[pl.ds(pl.multiple_of(base, 8), TILE_DEV), :] = blocks[k, core, xs, ys].astype(F32)

    def from_sibling(way, step, q, k):
        part = piece(k, 1 - c, q)
        rcopy(part, part, sib_s.at[0], sib_r.at[way, step, q], sibling).wait_recv()
        widen(k, 1 - c, q)

    last = NZ // 2
    for q in range(NQ):
        for xs in range(q * XQ, (q + 1) * XQ):
            part = blocks.at[z, c, xs]
            rcopy(part, part, scat_s.at[0], scat_r.at[xs], sibling).wait_recv()
        ring(0, 0, q, z)
        ring(1, 0, q, z)
        pass_on(0, 0, q, z)

    pltpu.make_async_copy(fetch_v, lists_v.at[me], own_sem.at[0]).wait()
    others = lists_v.at[pl.ds(0, NX * NY - 1)]
    rcopy(others, others, list_s.at[0], list_r.at[0], sibling).wait_recv()
    pltpu.make_async_copy(lists_v, lists_s, own_sem.at[2]).start()
    others = idx1.at[pl.ds(0, NZ - 1)]
    rcopy(others, others, id1_s.at[0], id1_r.at[0], sibling).wait_recv()
    for d in range(1, NX * NC):
        rcopy(idx1, idx2.at[xc], id2_s.at[0], id2_r.at[0], across(d)[1]).start()
    idx2[xc] = idx1[...]
    for q in range(NQ):
        widen(z, c, q)

    events = []
    for step in range(1, last + 1):
        for q in range(NQ):
            for way in range(2):
                if step < last or q == way:
                    events.append((way, step, q))
    pending = [(0, 0, q, z) for q in range(NQ)]
    for way, step, q in events:
        k = lax.rem(z + NZ - step, NZ) if way == 0 else lax.rem(z + step, NZ)
        part = piece(k, c, q)
        rcopy(part, part, ring_s.at[0], ring_r.at[way, step - 1, q], sibling).wait_recv()
        if step < last - 1 or (step == last - 1 and q == way):
            ring(way, step, q, k)
        pass_on(way, step, q, k)
        widen(k, c, q)
        pending.append((way, step, q, k))
        if len(pending) > 3:
            from_sibling(*pending.pop(0))
    pltpu.make_async_copy(lists_v, lists_s, own_sem.at[2]).wait()
    for item in pending:
        from_sibling(*item)

    def pick(t):
        for h in range(GHOSTS):
            stage[pl.ds(h, 1), :] = rows_f[pl.ds(lists_s[t, 0, h], 1), :]
        return stage[...].astype(BF)

    stage[pl.ds(GHOSTS - 2, GHOSTP - GHOSTS + 2), :] = jnp.zeros((GHOSTP - GHOSTS + 2, ROWS), F32)

    @pl.loop(1, NX * NY)
    def _(p):
        tx, ty = lax.rem(x + p // NY, NX), lax.rem(y + lax.rem(p, NY), NY)
        t = tx * NY + ty
        msg[t] = pick(t)
        rcopy(msg.at[t], got.at[me], ex_s.at[0], ex_r.at[0], dev(z, tx, c, ty)).start()

    got[me] = pick(me)

    place = lax.broadcasted_iota(jnp.int32, (OUT_ROWS, TILE_DEV * SLOTP), 0)
    seg[...] = (place == slots).astype(F32).astype(BF)
    others = idx2.at[pl.ds(0, NX * NC - 1)]
    rcopy(others, others, id2_s.at[0], id2_r.at[0], sibling).wait_recv()
    wanted = idx2[...].reshape(GROUPS * 8, 128)
    lanes = lax.broadcasted_iota(jnp.int32, (GROUPS * 8, 128), 1)
    chosen = jnp.sum(jnp.where(lanes == s, wanted, 0).astype(F32), axis=1, keepdims=True)
    target[...] = (lanes.astype(F32) == chosen).astype(F32).T.astype(BF)

    pltpu.make_async_copy(modes, mine, own_sem.at[1]).wait()
    others = table.at[pl.ds(0, (NY - 1) * TILE_DEV)]
    rcopy(others, others, all_s.at[0], all_r.at[0], sibling).wait_recv()
    others = got.at[pl.ds(0, NX * NY - 1)]
    rcopy(others, others, ex_s.at[0], ex_r.at[0], sibling).wait_recv()
    for m in range(MODES):
        got_f[pl.ds(m * GHOSTP, GHOSTP), :] = got[m].astype(F32)
    for h in range(GHOSTS):
        table[GROUP + h] = got_f[pl.ds(h, MODES, stride=GHOSTP), :].astype(BF)

    eye = lax.broadcasted_iota(jnp.int32, (ROWS, ROWS), 0) == lax.broadcasted_iota(
        jnp.int32, (ROWS, ROWS), 1
    )
    n = SLOTS * MODES
    same_slot = (
        lax.broadcasted_iota(jnp.int32, (n, n), 0) // MODES
        == lax.broadcasted_iota(jnp.int32, (n, n), 1) // MODES
    )
    spread = (
        lax.rem(lax.broadcasted_iota(jnp.int32, (n, MODES * MODES), 0), MODES)
        == lax.rem(lax.broadcasted_iota(jnp.int32, (n, MODES * MODES), 1), MODES)
    ).astype(F32).astype(BF)
    same_mode = (
        lax.rem(lax.broadcasted_iota(jnp.int32, (n, MODES * MODES), 0), MODES)
        == lax.broadcasted_iota(jnp.int32, (n, MODES * MODES), 1) // MODES
    )
    fold = (
        lax.broadcasted_iota(jnp.int32, (SLOTP, n), 0)
        == lax.broadcasted_iota(jnp.int32, (SLOTP, n), 1) // MODES
    ).astype(F32).astype(BF)

    @pl.loop(0, TILE_DEV)
    def _(t):
        pltpu.make_async_copy(a_hbm.at[t], a_v.at[t], a_sem.at[t]).wait()
        diagonal = jnp.sum(jnp.where(eye, a_v[t, 0].astype(F32), 0.0), axis=0, keepdims=True)
        scale = DAMPING / diagonal
        for k in range(SLOTS):
            column = table[col_s[0, t * SLOTP + k]]
            product = dot_t(column, a_v[t, k])
            value = -scale * product
            if k == 0:
                value = modes[t].astype(F32) + value
            pv[t, k] = value.astype(BF)
            qv[k] = product.astype(BF)
        both = dot_t(pv[t].reshape(n, ROWS), qv[...].reshape(n, ROWS)) * (1.0 / ROWS)
        both = jnp.where(same_slot, both, 0.0).astype(BF)
        wide = jnp.dot(both, spread, preferred_element_type=F32)
        wide = jnp.where(same_mode, wide, 0.0).astype(BF)
        flat[pl.ds(pl.multiple_of(t * SLOTP, SLOTP), SLOTP), :] = jnp.dot(
            fold, wide, preferred_element_type=F32
        ).astype(BF)

    pltpu.make_async_copy(pv, prolong, p_sem.at[0]).start()

    sums = jnp.dot(seg[...], flat[...], preferred_element_type=F32)
    out[...] = sums[GROUP:].astype(BF).reshape(NZ, NX * NC, 8, MODES * MODES)
    for d in range(1, NZ):
        tz, device = along_z(d)
        rcopy(out.at[tz], in1.at[z], c1_s.at[0], c1_r.at[0], device).start()
    in1[z] = out[z]
    others = in1.at[pl.ds(0, NZ - 1)]
    rcopy(others, others, c1_s.at[0], c1_r.at[0], sibling).wait_recv()
    for d in range(1, NX * NC):
        t, device = across(d)
        rcopy(in1.at[:, t], in2.at[xc], c2_s.at[0], c2_r.at[0], device).start()
    in2[xc] = in1[:, xc]
    others = in2.at[pl.ds(0, NX * NC - 1)]
    rcopy(others, others, c2_s.at[0], c2_r.at[0], sibling).wait_recv()
    returned = jnp.dot(
        target[...], in2[...].reshape(GROUPS * 8, MODES * MODES), preferred_element_type=F32
    )
    ysum[y] = (sums[:GROUP] + returned[:GROUP]).astype(BF)
    for d in range(1, NY):
        rcopy(ysum.at[y], ysum.at[y], y_s.at[0], y_r.at[0], along_y(d)).start()
    others = ysum.at[pl.ds(0, NY - 1)]
    rcopy(others, others, y_s.at[0], y_r.at[0], sibling).wait_recv()
    total = ysum[0].astype(F32)
    for k in range(1, NY):
        total = total + ysum[k].astype(F32)
    coarse[...] = total

    def sent(region, sem):
        rcopy(region, region, sem, sem, sibling).wait_send()

    sent(s1.at[pl.ds(0, NX * NY - 1)], scat_s.at[0])
    sent(lists_v.at[pl.ds(0, NX * NY - 1)], list_s.at[0])
    sent(idx1.at[pl.ds(0, NZ - 1)], id1_s.at[0])
    sent(idx2.at[pl.ds(0, NX * NC - 1)], id2_s.at[0])
    sent(table.at[pl.ds(0, (NY - 1) * TILE_DEV)], all_s.at[0])
    sent(blocks.at[pl.ds(0, NZ - 1), c], ring_s.at[0])
    sent(blocks.at[:, c], sib_s.at[0])
    sent(msg.at[pl.ds(0, NX * NY - 1)], ex_s.at[0])
    sent(out.at[pl.ds(0, NZ - 1)], c1_s.at[0])
    sent(in2.at[pl.ds(0, NX * NC - 1)], c2_s.at[0])
    sent(ysum.at[pl.ds(0, NY - 1)], y_s.at[0])
    pltpu.make_async_copy(pv, prolong, p_sem.at[0]).wait()


def shards(a_tiles, modes, col_tiles, fetch_list):
    fetch = jnp.pad(fetch_list, ((0, 0), (0, LIST - GHOSTS)))
    cols = jnp.pad(col_tiles, ((0, 0), (0, SLOTP - SLOTS)), constant_values=-1).reshape(1, TILE_DEV * SLOTP)
    dma = pltpu.SemaphoreType.DMA
    vmem = pl.BlockSpec(memory_space=pltpu.VMEM)
    smem = pl.BlockSpec(memory_space=pltpu.SMEM)
    hbm = pl.BlockSpec(memory_space=pl.ANY)
    plane = NX * NY
    one = dma((1,))
    prolong, coarse = pl.pallas_call(
        body,
        out_shape=(
            jax.ShapeDtypeStruct((TILE_DEV, SLOTS, MODES, ROWS), BF),
            jax.ShapeDtypeStruct((GROUP, MODES * MODES), F32),
        ),
        in_specs=[vmem, vmem, smem, smem, vmem, hbm],
        out_specs=(hbm, vmem),
        scratch_shapes=[
            pltpu.VMEM((TILE_DEV, SLOTS, ROWS, ROWS), BF),
            pltpu.VMEM((TILE_DEV * MODES, ROWS), F32),
            pltpu.VMEM((MODES, TILE_DEV, ROWS), BF),
            pltpu.VMEM((NZ, NC, NX, NY, TILE_DEV, ROWS), BF),
            pltpu.VMEM((TILES, ROWS), F32),
            pltpu.VMEM((plane, 1, LIST), jnp.int32),
            pltpu.SMEM((plane, 1, LIST), jnp.int32),
            pltpu.VMEM((GHOSTP, ROWS), F32),
            pltpu.VMEM((plane, GHOSTP, ROWS), BF),
            pltpu.VMEM((plane, GHOSTP, ROWS), BF),
            pltpu.VMEM((plane * GHOSTP, ROWS), F32),
            pltpu.VMEM((GROUP + GHOSTS, MODES, ROWS), BF),
            pltpu.VMEM((TILE_DEV, SLOTS, MODES, ROWS), BF),
            pltpu.VMEM((SLOTS, MODES, ROWS), BF),
            pltpu.VMEM((TILE_DEV * SLOTP, MODES * MODES), BF),
            pltpu.VMEM((OUT_ROWS, TILE_DEV * SLOTP), BF),
            pltpu.VMEM((8, 128), jnp.int32),
            pltpu.VMEM((NZ, 8, 128), jnp.int32),
            pltpu.VMEM((NX * NC, NZ, 8, 128), jnp.int32),
            pltpu.VMEM((128, GROUPS * 8), BF),
            pltpu.VMEM((NZ, NX * NC, 8, MODES * MODES), BF),
            pltpu.VMEM((NZ, NX * NC, 8, MODES * MODES), BF),
            pltpu.VMEM((NX * NC, NZ, 8, MODES * MODES), BF),
            pltpu.VMEM((NY, GROUP, MODES * MODES), BF),
            dma((TILE_DEV,)),
            one, dma((NX,)),
            one, one,
            dma((3,)),
            one, one,
            one, dma((2, NZ // 2, NQ)),
            one, dma((2, NZ // 2 + 1, NQ)),
            one, one,
            one, one, one, one,
            one, one, one, one,
            one, one,
            one,
        ],
        compiler_params=pltpu.CompilerParams(
            collective_id=0, has_side_effects=True, vmem_limit_bytes=56 * 2**20
        ),
    )(modes, fetch, fetch, cols, cols, a_tiles)
    return prolong, coarse


def solution(mesh):
    in_specs = (
        P(("sub", "blk"), None, None, None),
        P(("sub", "blk"), None, None),
        P(("sub", "blk"), None),
        P(("sub", "blk"), None),
    )
    out_specs = (P(("sub", "blk"), None, None, None), P("sub", None))
    return jax.shard_map(shards, mesh=mesh, in_specs=in_specs, out_specs=out_specs, check_vma=False)
```

```python
import functools

import jax
import jax.numpy as jnp
from jax import lax
from jax.experimental import pallas as pl
from jax.experimental.pallas import tpu as pltpu
from jax.sharding import PartitionSpec as P

MESH = pl.DeviceIdType.MESH
BF = jnp.bfloat16
F32 = jnp.float32
NZ, NX, NC, NY = 8, 4, 2, 4
TILE_DEV = 24
SLOTS = 12
SLOTP = 16
TP = 32
ROWS = 128
MODES = 16
GROUP = 96
GROUPS = NZ * NX * NC
TILES = GROUP * GROUPS
PER_PEER = 5
GHOSTS = 130
GHOSTP = 144
LIST = 256
NQ = 4
XQ = NX // NQ
OUT_ROWS = GROUP + GROUPS * 8
DAMPING = 2.0 / 3.0


def dev(z, x, c, y):
    return ((z * NX + x) * NC + c, y)


def rcopy(src, dst, send, recv, device):
    return pltpu.make_async_remote_copy(
        src_ref=src, dst_ref=dst, send_sem=send, recv_sem=recv, device_id=device, device_id_type=MESH
    )


def dot_t(a, b):
    return lax.dot_general(a, b, (((1,), (1,)), ((), ())), preferred_element_type=F32)


def body(
    modes, fetch_in, fetch_s, col_s, col_v, a_hbm, prolong, coarse,
    fetch_v, col_f, a_v, mf, s1, blocks, rows_f, lists_v, lists_s, stage, msg, got, got_f, table,
    pv, qv, flat, seg, req, idx1, idx2, target, out, back, ysum,
    a_sem, scat_s, scat_r, list_s, list_r, own_sem, all_s, all_r, ring_s, ring_r, sib_s, sib_r,
    ex_s, ex_r, id1_s, id1_r, id2_s, id2_r, c1_s, c1_r, y_s, y_r, p_sem,
):
    s = lax.axis_index("sub")
    y = lax.axis_index("blk")
    z, x, c = s // (NX * NC), lax.rem(s // NC, NX), lax.rem(s, NC)
    me = x * NY + y
    xc = x * NC + c
    right, left = dev(lax.rem(z + 1, NZ), x, c, y), dev(lax.rem(z + NZ - 1, NZ), x, c, y)
    sibling = dev(z, x, 1 - c, y)

    def plane(p):
        tx, ty = lax.rem(x + p // NY, NX), lax.rem(y + p % NY, NY)
        return tx * NY + ty, dev(z, tx, c, ty)

    def along_z(d):
        tz = lax.rem(z + d, NZ)
        return tz, dev(tz, x, c, y)

    def across(d):
        t = lax.rem(xc + d, NX * NC)
        return t, (z * NX * NC + t, y)

    def along_y(d):
        return dev(z, x, c, lax.rem(y + d, NY))

    barrier = pltpu.get_barrier_semaphore()
    partners = [plane(p)[1] for p in range(1, NX * NY)]
    partners += [along_z(d)[1] for d in range(1, NZ)]
    partners += [dev(z, lax.rem(x + d, NX), 1 - c, y) for d in range(NX)]
    for partner in partners:
        pl.semaphore_signal(barrier, inc=1, device_id=partner, device_id_type=MESH)

    mf[...] = modes[...].astype(F32).reshape(TILE_DEV * MODES, ROWS)
    for m in range(MODES):
        s1[m] = mf[pl.ds(m, TILE_DEV, stride=MODES), :].astype(BF)

    lane = lax.broadcasted_iota(jnp.int32, (8, 128), 1)
    sub8 = lax.broadcasted_iota(jnp.int32, (8, 128), 0)
    request = jnp.full((8, 128), -1, jnp.int32)
    slots = col_v[...]
    colvec = slots
    fetch_v[...] = jnp.zeros((1, LIST), jnp.int32)
    fetch_v[:, :GHOSTS] = fetch_in[...]
    for h in range(GHOSTS):
        tile = fetch_s[0, h]
        group = tile // GROUP
        request = jnp.where(
            (lane == group) & (sub8 == h % PER_PEER), tile - group * GROUP, request
        )
        slots = jnp.where(colvec == GROUP + h, GROUP + group * 8 + h % PER_PEER, slots)
    req[...] = request
    col_f[...] = jnp.full((SLOTP, 128), -1, jnp.int32)
    col_f[:SLOTS, :TILE_DEV] = slots
    lane1 = lax.broadcasted_iota(jnp.int32, (1, 128), 1)
    rows = []
    for k0 in range(0, SLOTS, 4):
        row = col_f[k0 : k0 + 1, :]
        for j in range(1, 4):
            row = jnp.where(lane1 // TP == j, pltpu.roll(col_f[k0 + j : k0 + j + 1, :], TP * j, 1), row)
        rows.append(row)
    slots = jnp.concatenate(rows, axis=1)
    flat[...] = jnp.zeros((2 * SLOTS * TP, 128), F32)

    pl.semaphore_wait(barrier, len(partners))

    pltpu.make_async_copy(s1.at[me], blocks.at[z, c, x, y], scat_r.at[x]).start()
    for p in range(1, NX * NY):
        t, device = plane(p)
        rcopy(s1.at[t], blocks.at[z, c, x, y], scat_s.at[0], scat_r.at[x], device).start()
    def piece(k, core, q):
        return blocks.at[k, core, pl.ds(q * XQ, XQ)]

    def ring(way, step, q, k):
        part = piece(k, c, q)
        device = right if way == 0 else left
        rcopy(part, part, ring_s.at[0], ring_r.at[way, step, q], device).start()

    def pass_on(way, step, q, k):
        part = piece(k, c, q)
        rcopy(part, part, sib_s.at[0], sib_r.at[way, step, q], sibling).start()

    def widen(k, core, q):
        for i in range(XQ * NY):
            xs, ys = q * XQ + i // NY, i % NY
            base = ((k * NX + xs) * NC + core) * GROUP + ys * TILE_DEV
            rows_f[pl.ds(pl.multiple_of(base, 8), TILE_DEV), :] = blocks[k, core, xs, ys].astype(F32)

    def from_sibling(way, step, q, k):
        part = piece(k, 1 - c, q)
        rcopy(part, part, sib_s.at[0], sib_r.at[way, step, q], sibling).wait_recv()
        widen(k, 1 - c, q)

    last = NZ // 2
    for q in range(NQ):
        for xs in range(q * XQ, (q + 1) * XQ):
            part = blocks.at[z, c, xs]
            rcopy(part, part, scat_s.at[0], scat_r.at[xs], sibling).wait_recv()
        ring(0, 0, q, z)
        ring(1, 0, q, z)
        pass_on(0, 0, q, z)

    for t in range(TILE_DEV):
        pltpu.make_async_copy(a_hbm.at[t], a_v.at[t], a_sem.at[t]).start()

    pltpu.make_async_copy(fetch_v, lists_v.at[me], own_sem.at[0]).start()
    for p in range(1, NX * NY):
        rcopy(fetch_v, lists_v.at[me], list_s.at[0], list_r.at[0], plane(p)[1]).start()
    for d in range(1, NZ):
        rcopy(req, idx1.at[z], id1_s.at[0], id1_r.at[0], along_z(d)[1]).start()
    mine = table.at[pl.ds(y * TILE_DEV, TILE_DEV)]
    pltpu.make_async_copy(modes, mine, own_sem.at[1]).start()
    for d in range(1, NY):
        rcopy(modes, mine, all_s.at[0], all_r.at[0], along_y(d)).start()
    idx1[z] = request

    for q in range(NQ):
        widen(z, c, q)

    def side_two():
        pltpu.make_async_copy(fetch_v, lists_v.at[me], own_sem.at[0]).wait()
        others = lists_v.at[pl.ds(0, NX * NY - 1)]
        rcopy(others, others, list_s.at[0], list_r.at[0], sibling).wait_recv()
        pltpu.make_async_copy(lists_v, lists_s, own_sem.at[2]).start()
        others = idx1.at[pl.ds(0, NZ - 1)]
        rcopy(others, others, id1_s.at[0], id1_r.at[0], sibling).wait_recv()
        for d in range(1, NX * NC):
            rcopy(idx1, idx2.at[xc], id2_s.at[0], id2_r.at[0], across(d)[1]).start()
        idx2[xc] = idx1[...]

    events = []
    for step in range(1, last + 1):
        for q in range(NQ):
            for way in range(2):
                if step < last or q * 2 // NQ == way:
                    events.append((way, step, q))
    pending = [(0, 0, q, z) for q in range(NQ)]
    for way, step, q in events:
        k = lax.rem(z + NZ - step, NZ) if way == 0 else lax.rem(z + step, NZ)
        part = piece(k, c, q)
        rcopy(part, part, ring_s.at[0], ring_r.at[way, step - 1, q], sibling).wait_recv()
        if step < last - 1 or (step == last - 1 and q * 2 // NQ == way):
            ring(way, step, q, k)
        pass_on(way, step, q, k)
        widen(k, c, q)
        pending.append((way, step, q, k))
        if (way, step, q) == (1, 2, NQ - 1):
            side_two()
        if len(pending) > 3:
            from_sibling(*pending.pop(0))
    pltpu.make_async_copy(lists_v, lists_s, own_sem.at[2]).wait()
    for item in pending:
        from_sibling(*item)

    def pick(t):
        for h in range(GHOSTS):
            stage[pl.ds(h, 1), :] = rows_f[pl.ds(lists_s[t, 0, h], 1), :]
        return stage[...].astype(BF)

    stage[pl.ds(GHOSTS - 2, GHOSTP - GHOSTS + 2), :] = jnp.zeros((GHOSTP - GHOSTS + 2, ROWS), F32)

    @pl.loop(1, NX * NY)
    def _(p):
        tx, ty = lax.rem(x + p // NY, NX), lax.rem(y + lax.rem(p, NY), NY)
        t = tx * NY + ty
        msg[t] = pick(t)
        rcopy(msg.at[t], got.at[me], ex_s.at[0], ex_r.at[0], dev(z, tx, c, ty)).start()

    got[me] = pick(me)

    place = lax.broadcasted_iota(jnp.int32, (OUT_ROWS, SLOTS * TP), 0)
    seg[...] = (place == slots).astype(F32).astype(BF)
    others = idx2.at[pl.ds(0, NX * NC - 1)]
    rcopy(others, others, id2_s.at[0], id2_r.at[0], sibling).wait_recv()
    wanted = jnp.concatenate([idx2[g % (NX * NC), g // (NX * NC)] for g in range(GROUPS)], axis=0)
    lanes = lax.broadcasted_iota(jnp.int32, (GROUPS * 8, 128), 1)
    chosen = jnp.sum(jnp.where(lanes == s, wanted, 0).astype(F32), axis=1, keepdims=True)
    target[...] = (lanes.astype(F32) == chosen).astype(F32).T.astype(BF)

    pltpu.make_async_copy(modes, mine, own_sem.at[1]).wait()
    others = table.at[pl.ds(0, (NY - 1) * TILE_DEV)]
    rcopy(others, others, all_s.at[0], all_r.at[0], sibling).wait_recv()
    others = got.at[pl.ds(0, NX * NY - 1)]
    rcopy(others, others, ex_s.at[0], ex_r.at[0], sibling).wait_recv()
    for m in range(MODES):
        got_f[pl.ds(m * GHOSTP, GHOSTP), :] = got[m].astype(F32)
    for h in range(GHOSTS):
        table[GROUP + h] = got_f[pl.ds(h, MODES, stride=GHOSTP), :].astype(BF)

    eye = lax.broadcasted_iota(jnp.int32, (ROWS, ROWS), 0) == lax.broadcasted_iota(
        jnp.int32, (ROWS, ROWS), 1
    )
    n = SLOTS * MODES
    same_slot = (
        lax.broadcasted_iota(jnp.int32, (n, n), 0) // MODES
        == lax.broadcasted_iota(jnp.int32, (n, n), 1) // MODES
    )
    spread = (
        lax.rem(lax.broadcasted_iota(jnp.int32, (n, MODES * MODES), 0), MODES)
        == lax.rem(lax.broadcasted_iota(jnp.int32, (n, MODES * MODES), 1), MODES)
    ).astype(F32).astype(BF)
    same_mode = (
        lax.rem(lax.broadcasted_iota(jnp.int32, (n, MODES * MODES), 0), MODES)
        == lax.broadcasted_iota(jnp.int32, (n, MODES * MODES), 1) // MODES
    )
    fold = (
        lax.broadcasted_iota(jnp.int32, (SLOTP, n), 0)
        == lax.broadcasted_iota(jnp.int32, (SLOTP, n), 1) // MODES
    ).astype(F32).astype(BF)

    def products(t):
        pltpu.make_async_copy(a_hbm.at[t], a_v.at[t], a_sem.at[t]).wait()
        diagonal = jnp.sum(jnp.where(eye, a_v[t, 0].astype(F32), 0.0), axis=0, keepdims=True)
        scale = DAMPING / diagonal
        for k in range(0, SLOTS, 2):
            columns = jnp.concatenate([table[col_s[k, t]], table[col_s[k + 1, t]]], axis=0)
            two = dot_t(columns, a_v[t, pl.ds(k, 2)].reshape(2 * ROWS, ROWS))
            parts = [two[:MODES, :ROWS], two[MODES:, ROWS:]]
            for j, product in enumerate(parts):
                value = -scale * product
                if k + j == 0:
                    value = modes[t].astype(F32) + value
                pv[t, k + j] = value.astype(BF)
                qv[t, k + j] = product.astype(BF)

    def pairs(t):
        both = dot_t(pv[t].reshape(n, ROWS), qv[t].reshape(n, ROWS)) * (1.0 / ROWS)
        return jnp.where(same_slot, both, 0.0).astype(BF)

    def widened(both):
        wide = jnp.dot(both, spread, preferred_element_type=F32)
        return jnp.where(same_mode, wide, 0.0)

    def folded(t, wide):
        res = jnp.dot(fold, wide.astype(BF), preferred_element_type=F32)
        flat[pl.ds(t, SLOTS, stride=TP), :] = res[:SLOTS, :128]
        flat[pl.ds(SLOTS * TP + t, SLOTS, stride=TP), :] = res[:SLOTS, 128:]

    @pl.loop(0, TILE_DEV, step=4)
    def _(t0):
        for u in range(4):
            products(t0 + u)

        bs = [pairs(t0 + u) for u in range(4)]
        ws = [widened(v) for v in bs]
        for u in range(4):
            folded(t0 + u, ws[u])

    pltpu.make_async_copy(pv, prolong, p_sem.at[0]).start()

    terms = jnp.concatenate([flat[: SLOTS * TP, :], flat[SLOTS * TP :, :]], axis=1).astype(BF)
    sums = jnp.dot(seg[...], terms, preferred_element_type=F32)
    out[...] = sums[GROUP:].astype(BF).reshape(GROUPS, 8, MODES * MODES)

    @pl.loop(1, GROUPS)
    def _(d):
        t = lax.rem(s + d, GROUPS)
        rcopy(out.at[t], back.at[s], c1_s.at[0], c1_r.at[0], (t, y)).start()

    back[s] = out[s]
    others = back.at[pl.ds(0, GROUPS - 1)]
    rcopy(others, others, c1_s.at[0], c1_r.at[0], sibling).wait_recv()
    returned = jnp.dot(
        target[...], back[...].reshape(GROUPS * 8, MODES * MODES), preferred_element_type=F32
    )
    ysum[y] = (sums[:GROUP] + returned[:GROUP]).astype(BF)
    for d in range(1, NY):
        rcopy(ysum.at[y], ysum.at[y], y_s.at[0], y_r.at[0], along_y(d)).start()
    others = ysum.at[pl.ds(0, NY - 1)]
    rcopy(others, others, y_s.at[0], y_r.at[0], sibling).wait_recv()
    total = ysum[0].astype(F32)
    for k in range(1, NY):
        total = total + ysum[k].astype(F32)
    coarse[...] = total

    def sent(region, sem):
        rcopy(region, region, sem, sem, sibling).wait_send()

    sent(s1.at[pl.ds(0, NX * NY - 1)], scat_s.at[0])
    sent(lists_v.at[pl.ds(0, NX * NY - 1)], list_s.at[0])
    sent(idx1.at[pl.ds(0, NZ - 1)], id1_s.at[0])
    sent(idx2.at[pl.ds(0, NX * NC - 1)], id2_s.at[0])
    sent(table.at[pl.ds(0, (NY - 1) * TILE_DEV)], all_s.at[0])
    sent(blocks.at[pl.ds(0, NZ - 1), c], ring_s.at[0])
    sent(blocks.at[:, c], sib_s.at[0])
    sent(msg.at[pl.ds(0, NX * NY - 1)], ex_s.at[0])
    sent(back.at[pl.ds(0, GROUPS - 1)], c1_s.at[0])
    sent(ysum.at[pl.ds(0, NY - 1)], y_s.at[0])
    pltpu.make_async_copy(pv, prolong, p_sem.at[0]).wait()


def shards(a_tiles, modes, col_tiles, fetch_list):
    cols = col_tiles.T
    dma = pltpu.SemaphoreType.DMA
    vmem = pl.BlockSpec(memory_space=pltpu.VMEM)
    smem = pl.BlockSpec(memory_space=pltpu.SMEM)
    hbm = pl.BlockSpec(memory_space=pl.ANY)
    plane = NX * NY
    one = dma((1,))
    prolong, coarse = pl.pallas_call(
        body,
        out_shape=(
            jax.ShapeDtypeStruct((TILE_DEV, SLOTS, MODES, ROWS), BF),
            jax.ShapeDtypeStruct((GROUP, MODES * MODES), F32),
        ),
        in_specs=[vmem, vmem, smem, smem, vmem, hbm],
        out_specs=(hbm, vmem),
        scratch_shapes=[
            pltpu.VMEM((1, LIST), jnp.int32),
            pltpu.VMEM((SLOTP, 128), jnp.int32),
            pltpu.VMEM((TILE_DEV, SLOTS, ROWS, ROWS), BF),
            pltpu.VMEM((TILE_DEV * MODES, ROWS), F32),
            pltpu.VMEM((MODES, TILE_DEV, ROWS), BF),
            pltpu.VMEM((NZ, NC, NX, NY, TILE_DEV, ROWS), BF),
            pltpu.VMEM((TILES, ROWS), F32),
            pltpu.VMEM((plane, 1, LIST), jnp.int32),
            pltpu.SMEM((plane, 1, LIST), jnp.int32),
            pltpu.VMEM((GHOSTP, ROWS), F32),
            pltpu.VMEM((plane, GHOSTP, ROWS), BF),
            pltpu.VMEM((plane, GHOSTP, ROWS), BF),
            pltpu.VMEM((plane * GHOSTP, ROWS), F32),
            pltpu.VMEM((GROUP + GHOSTS, MODES, ROWS), BF),
            pltpu.VMEM((TILE_DEV, SLOTS, MODES, ROWS), BF),
            pltpu.VMEM((TILE_DEV, SLOTS, MODES, ROWS), BF),
            pltpu.VMEM((2 * SLOTS * TP, 128), F32),
            pltpu.VMEM((OUT_ROWS, SLOTS * TP), BF),
            pltpu.VMEM((8, 128), jnp.int32),
            pltpu.VMEM((NZ, 8, 128), jnp.int32),
            pltpu.VMEM((NX * NC, NZ, 8, 128), jnp.int32),
            pltpu.VMEM((128, GROUPS * 8), BF),
            pltpu.VMEM((GROUPS, 8, MODES * MODES), BF),
            pltpu.VMEM((GROUPS, 8, MODES * MODES), BF),
            pltpu.VMEM((NY, GROUP, MODES * MODES), BF),
            dma((TILE_DEV,)),
            one, dma((NX,)),
            one, one,
            dma((3,)),
            one, one,
            one, dma((2, NZ // 2, NQ)),
            one, dma((2, NZ // 2 + 1, NQ)),
            one, one,
            one, one, one, one,
            one, one,
            one, one,
            one,
        ],
        compiler_params=pltpu.CompilerParams(
            collective_id=0, has_side_effects=True, vmem_limit_bytes=56 * 2**20
        ),
    )(modes, fetch_list, fetch_list, cols, cols, a_tiles)
    return prolong, coarse


def solution(mesh):
    in_specs = (
        P(("sub", "blk"), None, None, None),
        P(("sub", "blk"), None, None),
        P(("sub", "blk"), None),
        P(("sub", "blk"), None),
    )
    out_specs = (P(("sub", "blk"), None, None, None), P("sub", None))
    return jax.shard_map(shards, mesh=mesh, in_specs=in_specs, out_specs=out_specs, check_vma=False)
```

```python
import functools

import jax
import jax.numpy as jnp
from jax import lax
from jax.experimental import pallas as pl
from jax.experimental.pallas import tpu as pltpu
from jax.sharding import PartitionSpec as P

MESH = pl.DeviceIdType.MESH
BF = jnp.bfloat16
F32 = jnp.float32
NZ, NX, NC, NY = 8, 4, 2, 4
TILE_DEV = 24
SLOTS = 12
SLOTP = 16
TP = 32
ROWS = 128
MODES = 16
GROUP = 96
GROUPS = NZ * NX * NC
TILES = GROUP * GROUPS
PER_PEER = 5
GHOSTS = 130
GHOSTP = 144
LIST = 256
PARTS = 4
TOGETHER = 6
NQ = 4
XQ = NX // NQ
OUT_ROWS = GROUP + GROUPS * 8
DAMPING = 2.0 / 3.0


def dev(z, x, c, y):
    return ((z * NX + x) * NC + c, y)


def rcopy(src, dst, send, recv, device):
    return pltpu.make_async_remote_copy(
        src_ref=src, dst_ref=dst, send_sem=send, recv_sem=recv, device_id=device, device_id_type=MESH
    )


def dot_t(a, b):
    return lax.dot_general(a, b, (((1,), (1,)), ((), ())), preferred_element_type=F32)


def body(
    modes, fetch_in, fetch_s, col_s, col_v, a_hbm, prolong, coarse,
    fetch_v, col_f, a_v, mf, s1, blocks, rows_f, lists_v, lists_s, stage, msg, got, got_f, table,
    pv, qv, flat, seg, req, idx1, idx2, target, out, back, ysum, scales,
    a_sem, scat_s, scat_r, list_s, list_r, own_sem, all_s, all_r, ring_s, ring_r, sib_s, sib_r,
    ex_s, ex_r, id1_s, id1_r, id2_s, id2_r, c1_s, c1_r, y_s, y_r, p_sem,
):
    s = lax.axis_index("sub")
    y = lax.axis_index("blk")
    z, x, c = s // (NX * NC), lax.rem(s // NC, NX), lax.rem(s, NC)
    me = x * NY + y
    xc = x * NC + c
    right, left = dev(lax.rem(z + 1, NZ), x, c, y), dev(lax.rem(z + NZ - 1, NZ), x, c, y)
    sibling = dev(z, x, 1 - c, y)

    def plane(p):
        tx, ty = lax.rem(x + p // NY, NX), lax.rem(y + p % NY, NY)
        return tx * NY + ty, dev(z, tx, c, ty)

    def along_z(d):
        tz = lax.rem(z + d, NZ)
        return tz, dev(tz, x, c, y)

    def across(d):
        t = lax.rem(xc + d, NX * NC)
        return t, (z * NX * NC + t, y)

    def along_y(d):
        return dev(z, x, c, lax.rem(y + d, NY))

    barrier = pltpu.get_barrier_semaphore()
    partners = [plane(p)[1] for p in range(1, NX * NY)]
    partners += [along_z(d)[1] for d in range(1, NZ)]
    partners += [dev(z, lax.rem(x + d, NX), 1 - c, y) for d in range(NX)]
    for partner in partners:
        pl.semaphore_signal(barrier, inc=1, device_id=partner, device_id_type=MESH)

    mf[...] = modes[...].astype(F32).reshape(TILE_DEV * MODES, ROWS)
    for m in range(MODES):
        s1[m] = mf[pl.ds(m, TILE_DEV, stride=MODES), :].astype(BF)

    lane = lax.broadcasted_iota(jnp.int32, (8, 128), 1)
    sub8 = lax.broadcasted_iota(jnp.int32, (8, 128), 0)
    request = jnp.full((8, 128), -1, jnp.int32)
    slots = col_v[...]
    colvec = slots
    fetch_v[...] = jnp.zeros((1, LIST), jnp.int32)
    fetch_v[:, :GHOSTS] = fetch_in[...]
    for h in range(GHOSTS):
        tile = fetch_s[0, h]
        group = tile // GROUP
        request = jnp.where(
            (lane == group) & (sub8 == h % PER_PEER), tile - group * GROUP, request
        )
        slots = jnp.where(colvec == GROUP + h, GROUP + group * 8 + h % PER_PEER, slots)
    req[...] = request
    col_f[...] = jnp.full((SLOTP, 128), -1, jnp.int32)
    col_f[:SLOTS, :TILE_DEV] = slots
    lane1 = lax.broadcasted_iota(jnp.int32, (1, 128), 1)
    rows = []
    for k0 in range(0, SLOTS, 4):
        row = col_f[k0 : k0 + 1, :]
        for j in range(1, 4):
            row = jnp.where(lane1 // TP == j, pltpu.roll(col_f[k0 + j : k0 + j + 1, :], TP * j, 1), row)
        rows.append(row)
    slots = jnp.concatenate(rows, axis=1)
    flat[...] = jnp.zeros((2 * SLOTS * TP, 128), F32)

    pl.semaphore_wait(barrier, len(partners))

    pltpu.make_async_copy(s1.at[me], blocks.at[z, c, x, y], scat_r.at[x]).start()
    for i in range(1, NX * NY):
        t, device = plane(i * 7 % (NX * NY))
        rcopy(s1.at[t], blocks.at[z, c, x, y], scat_s.at[0], scat_r.at[x], device).start()
    def piece(k, core, q):
        return blocks.at[k, core, pl.ds(q * XQ, XQ)]

    def ring(way, step, q, k):
        part = piece(k, c, q)
        device = right if way == 0 else left
        rcopy(part, part, ring_s.at[0], ring_r.at[way, step, q], device).start()

    def pass_on(way, step, q, k):
        part = piece(k, c, q)
        rcopy(part, part, sib_s.at[0], sib_r.at[way, step, q], sibling).start()

    def widen(k, core, q):
        for i in range(XQ * NY):
            xs, ys = q * XQ + i // NY, i % NY
            base = ((k * NX + xs) * NC + core) * GROUP + ys * TILE_DEV
            rows_f[pl.ds(pl.multiple_of(base, 8), TILE_DEV), :] = blocks[k, core, xs, ys].astype(F32)

    def from_sibling(way, step, q, k):
        part = piece(k, 1 - c, q)
        rcopy(part, part, sib_s.at[0], sib_r.at[way, step, q], sibling).wait_recv()
        widen(k, 1 - c, q)

    last = NZ // 2
    for q in range(NQ):
        for xs in range(q * XQ, (q + 1) * XQ):
            part = blocks.at[z, c, xs]
            rcopy(part, part, scat_s.at[0], scat_r.at[xs], sibling).wait_recv()
        ring(0, 0, q, z)
        ring(1, 0, q, z)
        pass_on(0, 0, q, z)

    for t in range(TILE_DEV):
        pltpu.make_async_copy(a_hbm.at[t], a_v.at[t], a_sem.at[t]).start()

    pltpu.make_async_copy(fetch_v, lists_v.at[me], own_sem.at[0]).start()
    for p in range(1, NX * NY):
        rcopy(fetch_v, lists_v.at[me], list_s.at[0], list_r.at[0], plane(p)[1]).start()
    for d in range(1, NZ):
        rcopy(req, idx1.at[z], id1_s.at[0], id1_r.at[0], along_z(d)[1]).start()
    mine = table.at[pl.ds(y * TILE_DEV, TILE_DEV)]
    pltpu.make_async_copy(modes, mine, own_sem.at[1]).start()
    for d in range(1, NY):
        rcopy(modes, mine, all_s.at[0], all_r.at[0], along_y(d)).start()
    idx1[z] = request

    for q in range(NQ):
        widen(z, c, q)

    def side_two():
        pltpu.make_async_copy(fetch_v, lists_v.at[me], own_sem.at[0]).wait()
        others = lists_v.at[pl.ds(0, NX * NY - 1)]
        rcopy(others, others, list_s.at[0], list_r.at[0], sibling).wait_recv()
        pltpu.make_async_copy(lists_v, lists_s, own_sem.at[2]).start()
        others = idx1.at[pl.ds(0, NZ - 1)]
        rcopy(others, others, id1_s.at[0], id1_r.at[0], sibling).wait_recv()
        for d in range(1, NX * NC):
            rcopy(idx1, idx2.at[xc], id2_s.at[0], id2_r.at[0], across(d)[1]).start()
        idx2[xc] = idx1[...]

    events = []
    for step in range(1, last + 1):
        for q in range(NQ):
            for way in range(2):
                if step < last or q * 2 // NQ == way:
                    events.append((way, step, q))
    pending = [(0, 0, q, z) for q in range(NQ)]
    for way, step, q in events:
        k = lax.rem(z + NZ - step, NZ) if way == 0 else lax.rem(z + step, NZ)
        part = piece(k, c, q)
        rcopy(part, part, ring_s.at[0], ring_r.at[way, step - 1, q], sibling).wait_recv()
        if step < last - 1 or (step == last - 1 and q * 2 // NQ == way):
            ring(way, step, q, k)
        pass_on(way, step, q, k)
        widen(k, c, q)
        pending.append((way, step, q, k))
        if (way, step, q) == (1, 2, NQ - 1):
            side_two()
        if len(pending) > 3:
            from_sibling(*pending.pop(0))
    pltpu.make_async_copy(lists_v, lists_s, own_sem.at[2]).wait()
    for item in pending:
        from_sibling(*item)

    def pick(t):
        for h in range(GHOSTS):
            stage[pl.ds(h, 1), :] = rows_f[pl.ds(lists_s[t, 0, h], 1), :]
        return stage[...].astype(BF)

    stage[pl.ds(GHOSTS - 2, GHOSTP - GHOSTS + 2), :] = jnp.zeros((GHOSTP - GHOSTS + 2, ROWS), F32)

    @pl.loop(1, NX * NY)
    def _(i):
        p = lax.rem(i * 7, NX * NY)
        tx, ty = lax.rem(x + p // NY, NX), lax.rem(y + lax.rem(p, NY), NY)
        t = tx * NY + ty
        msg[t] = pick(t)
        rcopy(msg.at[t], got.at[me], ex_s.at[0], ex_r.at[0], dev(z, tx, c, ty)).start()

    got[me] = pick(me)

    place = lax.broadcasted_iota(jnp.int32, (OUT_ROWS, SLOTS * TP), 0)
    seg[...] = (place == slots).astype(F32).astype(BF)
    others = idx2.at[pl.ds(0, NX * NC - 1)]
    rcopy(others, others, id2_s.at[0], id2_r.at[0], sibling).wait_recv()
    wanted = jnp.concatenate([idx2[g % (NX * NC), g // (NX * NC)] for g in range(GROUPS)], axis=0)
    lanes = lax.broadcasted_iota(jnp.int32, (GROUPS * 8, 128), 1)
    chosen = jnp.sum(jnp.where(lanes == s, wanted, 0).astype(F32), axis=1, keepdims=True)
    target[...] = (lanes.astype(F32) == chosen).astype(F32).T.astype(BF)

    eye = lax.broadcasted_iota(jnp.int32, (ROWS, ROWS), 0) == lax.broadcasted_iota(
        jnp.int32, (ROWS, ROWS), 1
    )

    @pl.loop(0, TILE_DEV, step=4)
    def _(t0):
        for t in range(4):
            pltpu.make_async_copy(a_hbm.at[t0 + t], a_v.at[t0 + t], a_sem.at[t0 + t]).wait()
        for t in range(4):
            diagonal = jnp.sum(jnp.where(eye, a_v[t0 + t, 0].astype(F32), 0.0), axis=0, keepdims=True)
            scales[t0 + t] = DAMPING / diagonal

    pltpu.make_async_copy(modes, mine, own_sem.at[1]).wait()
    others = table.at[pl.ds(0, (NY - 1) * TILE_DEV)]
    rcopy(others, others, all_s.at[0], all_r.at[0], sibling).wait_recv()
    others = got.at[pl.ds(0, NX * NY - 1)]
    rcopy(others, others, ex_s.at[0], ex_r.at[0], sibling).wait_recv()
    for m in range(MODES):
        got_f[pl.ds(m * GHOSTP, GHOSTP), :] = got[m].astype(F32)
    for h in range(GHOSTS):
        table[GROUP + h] = got_f[pl.ds(h, MODES, stride=GHOSTP), :].astype(BF)

    n = SLOTS * MODES
    same_slot = (
        lax.broadcasted_iota(jnp.int32, (n, n), 0) // MODES
        == lax.broadcasted_iota(jnp.int32, (n, n), 1) // MODES
    )
    spread = (
        lax.rem(lax.broadcasted_iota(jnp.int32, (n, MODES * MODES), 0), MODES)
        == lax.rem(lax.broadcasted_iota(jnp.int32, (n, MODES * MODES), 1), MODES)
    ).astype(F32).astype(BF)
    same_mode = (
        lax.rem(lax.broadcasted_iota(jnp.int32, (n, MODES * MODES), 0), MODES)
        == lax.broadcasted_iota(jnp.int32, (n, MODES * MODES), 1) // MODES
    )
    fold = (
        lax.broadcasted_iota(jnp.int32, (SLOTP, n), 0)
        == lax.broadcasted_iota(jnp.int32, (SLOTP, n), 1) // MODES
    ).astype(F32).astype(BF)

    def products(t):
        scale = scales[t]
        for k in range(0, SLOTS, 2):
            columns = jnp.concatenate([table[col_s[k, t]], table[col_s[k + 1, t]]], axis=0)
            two = dot_t(columns, a_v[t, pl.ds(k, 2)].reshape(2 * ROWS, ROWS))
            parts = [two[:MODES, :ROWS], two[MODES:, ROWS:]]
            for j, product in enumerate(parts):
                value = -scale * product
                if k + j == 0:
                    value = modes[t].astype(F32) + value
                pv[t, k + j] = value.astype(BF)
                qv[t, k + j] = product.astype(BF)

    def pairs(t):
        both = dot_t(pv[t].reshape(n, ROWS), qv[t].reshape(n, ROWS)) * (1.0 / ROWS)
        return jnp.where(same_slot, both, 0.0).astype(BF)

    def widened(both):
        wide = jnp.dot(both, spread, preferred_element_type=F32)
        return jnp.where(same_mode, wide, 0.0)

    def folded(t, wide):
        res = jnp.dot(fold, wide.astype(BF), preferred_element_type=F32)
        flat[pl.ds(t, SLOTS, stride=TP), :] = res[:SLOTS, :128]
        flat[pl.ds(SLOTS * TP + t, SLOTS, stride=TP), :] = res[:SLOTS, 128:]

    @pl.loop(0, TILE_DEV, step=TOGETHER)
    def _(t0):
        for u in range(TOGETHER):
            products(t0 + u)

        bs = [pairs(t0 + u) for u in range(TOGETHER)]
        ws = [widened(v) for v in bs]
        for u in range(TOGETHER):
            folded(t0 + u, ws[u])

    pltpu.make_async_copy(pv, prolong, p_sem.at[0]).start()

    terms = jnp.concatenate([flat[: SLOTS * TP, :], flat[SLOTS * TP :, :]], axis=1).astype(BF)
    sums = jnp.dot(seg[...], terms, preferred_element_type=F32)
    out[...] = sums[GROUP:].astype(BF).reshape(GROUPS, 8, MODES * MODES)

    @pl.loop(1, GROUPS)
    def _(d):
        t = lax.rem(s + d * 37, GROUPS)
        rcopy(out.at[t], back.at[s], c1_s.at[0], c1_r.at[0], (t, y)).start()

    back[s] = out[s]
    others = back.at[pl.ds(0, GROUPS - 1)]
    rcopy(others, others, c1_s.at[0], c1_r.at[0], sibling).wait_recv()
    returned = jnp.dot(
        target[...], back[...].reshape(GROUPS * 8, MODES * MODES), preferred_element_type=F32
    )
    ysum[y] = (sums[:GROUP] + returned[:GROUP]).astype(BF)
    for d in range(1, NY):
        rcopy(ysum.at[y], ysum.at[y], y_s.at[0], y_r.at[0], along_y(d)).start()
    others = ysum.at[pl.ds(0, NY - 1)]
    rcopy(others, others, y_s.at[0], y_r.at[0], sibling).wait_recv()
    total = ysum[0].astype(F32)
    for k in range(1, NY):
        total = total + ysum[k].astype(F32)
    coarse[...] = total

    def sent(region, sem):
        rcopy(region, region, sem, sem, sibling).wait_send()

    sent(s1.at[pl.ds(0, NX * NY - 1)], scat_s.at[0])
    sent(lists_v.at[pl.ds(0, NX * NY - 1)], list_s.at[0])
    sent(idx1.at[pl.ds(0, NZ - 1)], id1_s.at[0])
    sent(idx2.at[pl.ds(0, NX * NC - 1)], id2_s.at[0])
    sent(table.at[pl.ds(0, (NY - 1) * TILE_DEV)], all_s.at[0])
    sent(blocks.at[pl.ds(0, NZ - 1), c], ring_s.at[0])
    sent(blocks.at[:, c], sib_s.at[0])
    sent(msg.at[pl.ds(0, NX * NY - 1)], ex_s.at[0])
    sent(back.at[pl.ds(0, GROUPS - 1)], c1_s.at[0])
    sent(ysum.at[pl.ds(0, NY - 1)], y_s.at[0])
    pltpu.make_async_copy(pv, prolong, p_sem.at[0]).wait()


def settle(prolong_in, coarse_in, prolong, coarse, held, held_c, in_s, out_s):
    def parts(i):
        if i == PARTS:
            return coarse_in, held_c, coarse
        span = pl.ds(i * (TILE_DEV // PARTS), TILE_DEV // PARTS)
        return prolong_in.at[span], held.at[span], prolong.at[span]

    for i in range(PARTS + 1):
        src, mid, _ = parts(i)
        pltpu.make_async_copy(src, mid, in_s.at[i]).start()
    for i in range(PARTS + 1):
        src, mid, dst = parts(i)
        pltpu.make_async_copy(src, mid, in_s.at[i]).wait()
        pltpu.make_async_copy(mid, dst, out_s.at[i]).start()
    for i in range(PARTS + 1):
        _, mid, dst = parts(i)
        pltpu.make_async_copy(mid, dst, out_s.at[i]).wait()


def shards(a_tiles, modes, col_tiles, fetch_list):
    cols = col_tiles.T
    dma = pltpu.SemaphoreType.DMA
    vmem = pl.BlockSpec(memory_space=pltpu.VMEM)
    smem = pl.BlockSpec(memory_space=pltpu.SMEM)
    hbm = pl.BlockSpec(memory_space=pl.ANY)
    plane = NX * NY
    one = dma((1,))
    shapes = (
        jax.ShapeDtypeStruct((TILE_DEV, SLOTS, MODES, ROWS), BF),
        jax.ShapeDtypeStruct((GROUP, MODES * MODES), F32),
    )
    prolong, coarse = pl.pallas_call(
        body,
        out_shape=shapes,
        in_specs=[vmem, vmem, smem, smem, vmem, hbm],
        out_specs=(hbm, vmem),
        scratch_shapes=[
            pltpu.VMEM((1, LIST), jnp.int32),
            pltpu.VMEM((SLOTP, 128), jnp.int32),
            pltpu.VMEM((TILE_DEV, SLOTS, ROWS, ROWS), BF),
            pltpu.VMEM((TILE_DEV * MODES, ROWS), F32),
            pltpu.VMEM((MODES, TILE_DEV, ROWS), BF),
            pltpu.VMEM((NZ, NC, NX, NY, TILE_DEV, ROWS), BF),
            pltpu.VMEM((TILES, ROWS), F32),
            pltpu.VMEM((plane, 1, LIST), jnp.int32),
            pltpu.SMEM((plane, 1, LIST), jnp.int32),
            pltpu.VMEM((GHOSTP, ROWS), F32),
            pltpu.VMEM((plane, GHOSTP, ROWS), BF),
            pltpu.VMEM((plane, GHOSTP, ROWS), BF),
            pltpu.VMEM((plane * GHOSTP, ROWS), F32),
            pltpu.VMEM((GROUP + GHOSTS, MODES, ROWS), BF),
            pltpu.VMEM((TILE_DEV, SLOTS, MODES, ROWS), BF),
            pltpu.VMEM((TILE_DEV, SLOTS, MODES, ROWS), BF),
            pltpu.VMEM((2 * SLOTS * TP, 128), F32),
            pltpu.VMEM((OUT_ROWS, SLOTS * TP), BF),
            pltpu.VMEM((8, 128), jnp.int32),
            pltpu.VMEM((NZ, 8, 128), jnp.int32),
            pltpu.VMEM((NX * NC, NZ, 8, 128), jnp.int32),
            pltpu.VMEM((128, GROUPS * 8), BF),
            pltpu.VMEM((GROUPS, 8, MODES * MODES), BF),
            pltpu.VMEM((GROUPS, 8, MODES * MODES), BF),
            pltpu.VMEM((NY, GROUP, MODES * MODES), BF),
            pltpu.VMEM((TILE_DEV, 1, ROWS), F32),
            dma((TILE_DEV,)),
            one, dma((NX,)),
            one, one,
            dma((3,)),
            one, one,
            one, dma((2, NZ // 2, NQ)),
            one, dma((2, NZ // 2 + 1, NQ)),
            one, one,
            one, one, one, one,
            one, one,
            one, one,
            one,
        ],
        compiler_params=pltpu.CompilerParams(
            collective_id=0, has_side_effects=True, vmem_limit_bytes=56 * 2**20
        ),
    )(modes, fetch_list, fetch_list, cols, cols, a_tiles)
    return pl.pallas_call(
        settle,
        out_shape=shapes,
        in_specs=[hbm, hbm],
        out_specs=(hbm, hbm),
        scratch_shapes=[
            pltpu.VMEM((TILE_DEV, SLOTS, MODES, ROWS), BF),
            pltpu.VMEM((GROUP, MODES * MODES), F32),
            dma((PARTS + 1,)),
            dma((PARTS + 1,)),
        ],
    )(prolong, coarse)


def solution(mesh):
    in_specs = (
        P(("sub", "blk"), None, None, None),
        P(("sub", "blk"), None, None),
        P(("sub", "blk"), None),
        P(("sub", "blk"), None),
    )
    out_specs = (P(("sub", "blk"), None, None, None), P("sub", None))
    return jax.shard_map(shards, mesh=mesh, in_specs=in_specs, out_specs=out_specs, check_vma=False)
```

```python
import functools

import jax
import jax.numpy as jnp
from jax import lax
from jax.experimental import pallas as pl
from jax.experimental.pallas import tpu as pltpu
from jax.sharding import PartitionSpec as P

MESH = pl.DeviceIdType.MESH
BF = jnp.bfloat16
F32 = jnp.float32
NZ, NX, NC, NY = 8, 4, 2, 4
TILE_DEV = 24
SLOTS = 12
SLOTP = 16
TP = 32
ROWS = 128
MODES = 16
GROUP = 96
GROUPS = NZ * NX * NC
TILES = GROUP * GROUPS
PER_PEER = 5
GHOSTS = 130
GHOSTP = 144
LIST = 256
PARTS = 4
TOGETHER = 6
NQ = 4
PLANE = NX * NY
PQ = PLANE // NQ
OUT_ROWS = GROUP + GROUPS * 8
DAMPING = 2.0 / 3.0


def dev(z, x, c, y):
    return ((z * NX + x) * NC + c, y)


def rcopy(src, dst, send, recv, device):
    return pltpu.make_async_remote_copy(
        src_ref=src, dst_ref=dst, send_sem=send, recv_sem=recv, device_id=device, device_id_type=MESH
    )


def dot_t(a, b):
    return lax.dot_general(a, b, (((1,), (1,)), ((), ())), preferred_element_type=F32)


def body(
    modes, fetch_in, fetch_s, col_s, col_v, a_hbm, prolong, coarse,
    fetch_v, col_f, a_v, mf, s1, blocks, rows_f, lists_v, lists_s, stage, msg, got, got_f, table,
    pv, qv, flat, seg, req, idx1, idx2, target, out, back, pack, unpack, ysum, scales,
    a_sem, scat_s, scat_r, list_s, list_r, own_sem, all_s, all_r, ring_s, ring_r, sib_s, sib_r,
    ex_s, ex_r, id1_s, id1_r, id2_s, id2_r, c1_s, c1_r, y_s, y_r, p_sem,
):
    s = lax.axis_index("sub")
    y = lax.axis_index("blk")
    z, x, c = s // (NX * NC), lax.rem(s // NC, NX), lax.rem(s, NC)
    me = x * NY + y
    xc = x * NC + c
    right, left = dev(lax.rem(z + 1, NZ), x, c, y), dev(lax.rem(z + NZ - 1, NZ), x, c, y)
    sibling = dev(z, x, 1 - c, y)

    def plane(p, d=0):
        tx, ty = lax.rem(x + p // NY, NX), lax.rem(y + p % NY, NY)
        return tx * NY + ty, dev(lax.rem(z + d, NZ), tx, c, ty)

    def along_z(d):
        tz = lax.rem(z + d, NZ)
        return tz, dev(tz, x, c, y)

    def across(d):
        t = lax.rem(xc + d, NX * NC)
        return t, (z * NX * NC + t, y)

    def along_y(d):
        return dev(z, x, c, lax.rem(y + d, NY))

    barrier = pltpu.get_barrier_semaphore()
    partners = [plane(p, d)[1] for d in (0, 1, NZ - 1) for p in range(PLANE) if p or d]
    partners += [along_z(d)[1] for d in range(2, NZ - 1)]
    partners += [dev(z, lax.rem(x + d, NX), 1 - c, y) for d in range(NX)]
    for partner in partners:
        pl.semaphore_signal(barrier, inc=1, device_id=partner, device_id_type=MESH)

    mf[...] = modes[...].astype(F32).reshape(TILE_DEV * MODES, ROWS)
    for m in range(MODES):
        s1[m] = mf[pl.ds(m, TILE_DEV, stride=MODES), :].astype(BF)

    pl.semaphore_wait(barrier, len(partners))

    pltpu.make_async_copy(s1.at[me], blocks.at[z, c, me], scat_r.at[0, me // PQ]).start()
    for i in range(PLANE):
        for j, d in ((1, 1), (2, NZ - 1), (0, 0)):
            if i or d:
                t, device = plane(i * 7 % PLANE, d)
                rcopy(s1.at[t], blocks.at[z, c, me], scat_s.at[j], scat_r.at[j, me // PQ], device).start()

    def piece(k, core, q):
        return blocks.at[k, core, pl.ds(q * PQ, PQ)]

    def ring(way, step, q, k):
        part = piece(k, c, q)
        device = right if way == 0 else left
        rcopy(part, part, ring_s.at[0], ring_r.at[way, step - 1, q], device).start()

    def pass_on(way, step, q, k):
        part = piece(k, c, q)
        rcopy(part, part, sib_s.at[0], sib_r.at[way, step, q], sibling).start()

    def widen(k, core, q):
        for u in range(q * PQ, (q + 1) * PQ):
            base = ((k * NX + u // NY) * NC + core) * GROUP + u % NY * TILE_DEV
            rows_f[pl.ds(pl.multiple_of(base, 8), TILE_DEV), :] = blocks[k, core, u].astype(F32)

    def from_sibling(way, step, q, k):
        part = piece(k, 1 - c, q)
        rcopy(part, part, sib_s.at[0], sib_r.at[way, step, q], sibling).wait_recv()
        widen(k, 1 - c, q)

    last = NZ // 2

    def arrived(j, q, k):
        part = piece(k, c, q)
        rcopy(part, part, scat_s.at[0], scat_r.at[j, q], sibling).wait_recv()

    for q in range(NQ):
        for way in range(2):
            k = lax.rem(z + (NZ - 1, 1)[way], NZ)
            arrived(1 + way, q, k)
            ring(way, 1, q, k)
            pass_on(way, 1, q, k)
    for q in range(NQ):
        arrived(0, q, z)
        pass_on(0, 0, q, z)

    for t in range(TILE_DEV):
        pltpu.make_async_copy(a_hbm.at[t], a_v.at[t], a_sem.at[t]).start()

    lane = lax.broadcasted_iota(jnp.int32, (8, 128), 1)
    sub8 = lax.broadcasted_iota(jnp.int32, (8, 128), 0)
    request = jnp.full((8, 128), -1, jnp.int32)
    slots = col_v[...]
    colvec = slots
    fetch_v[...] = jnp.zeros((1, LIST), jnp.int32)
    fetch_v[:, :GHOSTS] = fetch_in[...]
    for h in range(GHOSTS):
        tile = fetch_s[0, h]
        group = tile // GROUP
        request = jnp.where(
            (lane == group) & (sub8 == h % PER_PEER), tile - group * GROUP, request
        )
        slots = jnp.where(colvec == GROUP + h, GROUP + group * 8 + h % PER_PEER, slots)
    req[...] = request
    col_f[...] = jnp.full((SLOTP, 128), -1, jnp.int32)
    col_f[:SLOTS, :TILE_DEV] = slots
    lane1 = lax.broadcasted_iota(jnp.int32, (1, 128), 1)
    rows = []
    for k0 in range(0, SLOTS, 4):
        row = col_f[k0 : k0 + 1, :]
        for j in range(1, 4):
            row = jnp.where(lane1 // TP == j, pltpu.roll(col_f[k0 + j : k0 + j + 1, :], TP * j, 1), row)
        rows.append(row)
    slots = jnp.concatenate(rows, axis=1)
    flat[...] = jnp.zeros((2 * SLOTS * TP, 128), F32)

    pltpu.make_async_copy(fetch_v, lists_v.at[me], own_sem.at[0]).start()
    for p in range(1, NX * NY):
        rcopy(fetch_v, lists_v.at[me], list_s.at[0], list_r.at[0], plane(p)[1]).start()
    for d in range(1, NZ):
        rcopy(req, idx1.at[z], id1_s.at[0], id1_r.at[0], along_z(d)[1]).start()
    mine = table.at[pl.ds(y * TILE_DEV, TILE_DEV)]
    pltpu.make_async_copy(modes, mine, own_sem.at[1]).start()
    for d in range(1, NY):
        rcopy(modes, mine, all_s.at[0], all_r.at[0], along_y(d)).start()
    idx1[z] = request

    for q in range(NQ):
        widen(z, c, q)

    def side_two():
        pltpu.make_async_copy(fetch_v, lists_v.at[me], own_sem.at[0]).wait()
        others = lists_v.at[pl.ds(0, NX * NY - 1)]
        rcopy(others, others, list_s.at[0], list_r.at[0], sibling).wait_recv()
        pltpu.make_async_copy(lists_v, lists_s, own_sem.at[2]).start()
        others = idx1.at[pl.ds(0, NZ - 1)]
        rcopy(others, others, id1_s.at[0], id1_r.at[0], sibling).wait_recv()
        for d in range(1, NX * NC):
            rcopy(idx1, idx2.at[xc], id2_s.at[0], id2_r.at[0], across(d)[1]).start()
        idx2[xc] = idx1[...]

    events = []
    for step in range(2, last + 1):
        for q in range(NQ):
            for way in range(2):
                if step < last or q * 2 // NQ == way:
                    events.append((way, step, q))
    pending = [(0, 0, q, z) for q in range(NQ)]
    for q in range(NQ):
        for way in range(2):
            k = lax.rem(z + (NZ - 1, 1)[way], NZ)
            widen(k, c, q)
            pending.append((way, 1, q, k))
    for way, step, q in events:
        k = lax.rem(z + NZ - step, NZ) if way == 0 else lax.rem(z + step, NZ)
        part = piece(k, c, q)
        rcopy(part, part, ring_s.at[0], ring_r.at[way, step - 2, q], sibling).wait_recv()
        if step < last - 1 or (step == last - 1 and q * 2 // NQ == way):
            ring(way, step, q, k)
        pass_on(way, step, q, k)
        widen(k, c, q)
        pending.append((way, step, q, k))
        if (way, step, q) == (1, 2, NQ - 1):
            side_two()
        for _ in range(2):
            if len(pending) > 3:
                from_sibling(*pending.pop(0))
    pltpu.make_async_copy(lists_v, lists_s, own_sem.at[2]).wait()
    for item in pending:
        from_sibling(*item)

    def pick(t):
        for h in range(GHOSTS):
            stage[pl.ds(h, 1), :] = rows_f[pl.ds(lists_s[t, 0, h], 1), :]
        return stage[...].astype(BF)

    stage[pl.ds(GHOSTS - 2, GHOSTP - GHOSTS + 2), :] = jnp.zeros((GHOSTP - GHOSTS + 2, ROWS), F32)

    @pl.loop(1, NX * NY)
    def _(i):
        p = lax.rem(i * 7, NX * NY)
        tx, ty = lax.rem(x + p // NY, NX), lax.rem(y + lax.rem(p, NY), NY)
        t = tx * NY + ty
        msg[t] = pick(t)
        rcopy(msg.at[t], got.at[me], ex_s.at[0], ex_r.at[0], dev(z, tx, c, ty)).start()

    got[me] = pick(me)

    place = lax.broadcasted_iota(jnp.int32, (OUT_ROWS, SLOTS * TP), 0)
    seg[...] = (place == slots).astype(F32).astype(BF)
    others = idx2.at[pl.ds(0, NX * NC - 1)]
    rcopy(others, others, id2_s.at[0], id2_r.at[0], sibling).wait_recv()
    wanted = jnp.concatenate([idx2[g % (NX * NC), g // (NX * NC)] for g in range(GROUPS)], axis=0)
    lanes = lax.broadcasted_iota(jnp.int32, (GROUPS * 8, 128), 1)
    chosen = jnp.sum(jnp.where(lanes == s, wanted, 0).astype(F32), axis=1, keepdims=True)
    target[...] = (lanes.astype(F32) == chosen).astype(F32).T.astype(BF)

    full = MODES * MODES

    def pair(entry):
        m, n = entry // MODES, lax.rem(entry, MODES)
        high, low = jnp.maximum(m, n), jnp.minimum(m, n)
        return high * (high + 1) // 2 + low, m >= n

    def lane_pair(at):
        return jnp.where(at < 128, at, 128 + lax.rem(at, 8))

    down = lax.broadcasted_iota(jnp.int32, (full, full), 0)
    over = lax.broadcasted_iota(jnp.int32, (full, full), 1)
    index, kept = pair(down)
    pack[...] = ((index == lane_pair(over)) & kept).astype(F32).astype(BF)
    unpack[...] = (pair(over)[0] == lane_pair(down)).astype(F32).astype(BF)

    eye = lax.broadcasted_iota(jnp.int32, (ROWS, ROWS), 0) == lax.broadcasted_iota(
        jnp.int32, (ROWS, ROWS), 1
    )

    @pl.loop(0, TILE_DEV, step=4)
    def _(t0):
        for t in range(4):
            pltpu.make_async_copy(a_hbm.at[t0 + t], a_v.at[t0 + t], a_sem.at[t0 + t]).wait()
        for t in range(4):
            diagonal = jnp.sum(jnp.where(eye, a_v[t0 + t, 0].astype(F32), 0.0), axis=0, keepdims=True)
            scales[t0 + t] = DAMPING / diagonal

    pltpu.make_async_copy(modes, mine, own_sem.at[1]).wait()
    others = table.at[pl.ds(0, (NY - 1) * TILE_DEV)]
    rcopy(others, others, all_s.at[0], all_r.at[0], sibling).wait_recv()
    others = got.at[pl.ds(0, NX * NY - 1)]
    rcopy(others, others, ex_s.at[0], ex_r.at[0], sibling).wait_recv()
    for m in range(MODES):
        got_f[pl.ds(m * GHOSTP, GHOSTP), :] = got[m].astype(F32)
    for h in range(GHOSTS):
        table[GROUP + h] = got_f[pl.ds(h, MODES, stride=GHOSTP), :].astype(BF)

    n = SLOTS * MODES
    same_slot = (
        lax.broadcasted_iota(jnp.int32, (n, n), 0) // MODES
        == lax.broadcasted_iota(jnp.int32, (n, n), 1) // MODES
    )
    spread = (
        lax.rem(lax.broadcasted_iota(jnp.int32, (n, MODES * MODES), 0), MODES)
        == lax.rem(lax.broadcasted_iota(jnp.int32, (n, MODES * MODES), 1), MODES)
    ).astype(F32).astype(BF)
    same_mode = (
        lax.rem(lax.broadcasted_iota(jnp.int32, (n, MODES * MODES), 0), MODES)
        == lax.broadcasted_iota(jnp.int32, (n, MODES * MODES), 1) // MODES
    )
    fold = (
        lax.broadcasted_iota(jnp.int32, (SLOTP, n), 0)
        == lax.broadcasted_iota(jnp.int32, (SLOTP, n), 1) // MODES
    ).astype(F32).astype(BF)

    def products(t):
        scale = scales[t]
        for k in range(0, SLOTS, 2):
            columns = jnp.concatenate([table[col_s[k, t]], table[col_s[k + 1, t]]], axis=0)
            two = dot_t(columns, a_v[t, pl.ds(k, 2)].reshape(2 * ROWS, ROWS))
            parts = [two[:MODES, :ROWS], two[MODES:, ROWS:]]
            for j, product in enumerate(parts):
                value = -scale * product
                if k + j == 0:
                    value = modes[t].astype(F32) + value
                pv[t, k + j] = value.astype(BF)
                qv[t, k + j] = product.astype(BF)

    def pairs(t):
        both = dot_t(pv[t].reshape(n, ROWS), qv[t].reshape(n, ROWS)) * (1.0 / ROWS)
        return jnp.where(same_slot, both, 0.0).astype(BF)

    def widened(both):
        wide = jnp.dot(both, spread, preferred_element_type=F32)
        return jnp.where(same_mode, wide, 0.0)

    def folded(t, wide):
        res = jnp.dot(fold, wide.astype(BF), preferred_element_type=F32)
        flat[pl.ds(t, SLOTS, stride=TP), :] = res[:SLOTS, :128]
        flat[pl.ds(SLOTS * TP + t, SLOTS, stride=TP), :] = res[:SLOTS, 128:]

    @pl.loop(0, TILE_DEV, step=TOGETHER)
    def _(t0):
        for u in range(TOGETHER):
            products(t0 + u)

        bs = [pairs(t0 + u) for u in range(TOGETHER)]
        ws = [widened(v) for v in bs]
        for u in range(TOGETHER):
            folded(t0 + u, ws[u])

    pltpu.make_async_copy(pv, prolong, p_sem.at[0]).start()

    terms = jnp.concatenate([flat[: SLOTS * TP, :], flat[SLOTS * TP :, :]], axis=1).astype(BF)
    sums = jnp.dot(seg[...], terms, preferred_element_type=F32)
    packed = jnp.dot(sums[GROUP:].astype(BF), pack[...], preferred_element_type=F32)
    slot_row = lax.broadcasted_iota(jnp.int32, (GROUPS, 8, 128), 1)
    own_lanes = lax.broadcasted_iota(jnp.int32, (GROUPS, 8, 128), 2) // 8 == slot_row
    rest = jnp.where(own_lanes, packed[:, 128:].reshape(GROUPS, 8, 128), 0.0)
    rest = jnp.broadcast_to(jnp.sum(rest, axis=1, keepdims=True), (GROUPS, 8, 128))
    out[...] = jnp.where(slot_row == PER_PEER, rest, packed[:, :128].reshape(GROUPS, 8, 128)).astype(BF)

    @pl.loop(1, GROUPS)
    def _(d):
        t = lax.rem(s + d * 37, GROUPS)
        rcopy(out.at[t], back.at[s], c1_s.at[0], c1_r.at[0], (t, y)).start()

    back[s] = out[s]
    others = back.at[pl.ds(0, GROUPS - 1)]
    rcopy(others, others, c1_s.at[0], c1_r.at[0], sibling).wait_recv()
    came = back[...]
    rest = jnp.broadcast_to(came[:, PER_PEER : PER_PEER + 1, :].astype(F32), (GROUPS, 8, 128))
    rest = jnp.where(own_lanes, rest, 0.0).astype(BF)
    both = jnp.concatenate([came.reshape(GROUPS * 8, 128), rest.reshape(GROUPS * 8, 128)], axis=1)
    found = jnp.dot(target[...], both, preferred_element_type=F32)
    upper = found.astype(BF)
    lower = (found - upper.astype(F32)).astype(BF)
    returned = jnp.dot(upper, unpack[...], preferred_element_type=F32)
    returned = returned + jnp.dot(lower, unpack[...], preferred_element_type=F32)
    ysum[y] = (sums[:GROUP] + returned[:GROUP]).astype(BF)
    for d in range(1, NY):
        rcopy(ysum.at[y], ysum.at[y], y_s.at[0], y_r.at[0], along_y(d)).start()
    others = ysum.at[pl.ds(0, NY - 1)]
    rcopy(others, others, y_s.at[0], y_r.at[0], sibling).wait_recv()
    total = ysum[0].astype(F32)
    for k in range(1, NY):
        total = total + ysum[k].astype(F32)
    coarse[...] = total

    def sent(region, sem):
        rcopy(region, region, sem, sem, sibling).wait_send()

    sent(s1.at[pl.ds(0, PLANE - 1)], scat_s.at[0])
    sent(s1, scat_s.at[1])
    sent(s1, scat_s.at[2])
    sent(lists_v.at[pl.ds(0, NX * NY - 1)], list_s.at[0])
    sent(idx1.at[pl.ds(0, NZ - 1)], id1_s.at[0])
    sent(idx2.at[pl.ds(0, NX * NC - 1)], id2_s.at[0])
    sent(table.at[pl.ds(0, (NY - 1) * TILE_DEV)], all_s.at[0])
    sent(blocks.at[pl.ds(0, NZ - 3), c], ring_s.at[0])
    sent(blocks.at[:, c], sib_s.at[0])
    sent(msg.at[pl.ds(0, NX * NY - 1)], ex_s.at[0])
    sent(back.at[pl.ds(0, GROUPS - 1)], c1_s.at[0])
    sent(ysum.at[pl.ds(0, NY - 1)], y_s.at[0])
    pltpu.make_async_copy(pv, prolong, p_sem.at[0]).wait()


def settle(prolong_in, coarse_in, prolong, coarse, held, held_c, in_s, out_s):
    def parts(i):
        if i == PARTS:
            return coarse_in, held_c, coarse
        span = pl.ds(i * (TILE_DEV // PARTS), TILE_DEV // PARTS)
        return prolong_in.at[span], held.at[span], prolong.at[span]

    for i in range(PARTS + 1):
        src, mid, _ = parts(i)
        pltpu.make_async_copy(src, mid, in_s.at[i]).start()
    for i in range(PARTS + 1):
        src, mid, dst = parts(i)
        pltpu.make_async_copy(src, mid, in_s.at[i]).wait()
        pltpu.make_async_copy(mid, dst, out_s.at[i]).start()
    for i in range(PARTS + 1):
        _, mid, dst = parts(i)
        pltpu.make_async_copy(mid, dst, out_s.at[i]).wait()


def shards(a_tiles, modes, col_tiles, fetch_list):
    cols = col_tiles.T
    dma = pltpu.SemaphoreType.DMA
    vmem = pl.BlockSpec(memory_space=pltpu.VMEM)
    smem = pl.BlockSpec(memory_space=pltpu.SMEM)
    hbm = pl.BlockSpec(memory_space=pl.ANY)
    plane = NX * NY
    one = dma((1,))
    shapes = (
        jax.ShapeDtypeStruct((TILE_DEV, SLOTS, MODES, ROWS), BF),
        jax.ShapeDtypeStruct((GROUP, MODES * MODES), F32),
    )
    prolong, coarse = pl.pallas_call(
        body,
        out_shape=shapes,
        in_specs=[vmem, vmem, smem, smem, vmem, hbm],
        out_specs=(hbm, vmem),
        scratch_shapes=[
            pltpu.VMEM((1, LIST), jnp.int32),
            pltpu.VMEM((SLOTP, 128), jnp.int32),
            pltpu.VMEM((TILE_DEV, SLOTS, ROWS, ROWS), BF),
            pltpu.VMEM((TILE_DEV * MODES, ROWS), F32),
            pltpu.VMEM((MODES, TILE_DEV, ROWS), BF),
            pltpu.VMEM((NZ, NC, PLANE, TILE_DEV, ROWS), BF),
            pltpu.VMEM((TILES, ROWS), F32),
            pltpu.VMEM((plane, 1, LIST), jnp.int32),
            pltpu.SMEM((plane, 1, LIST), jnp.int32),
            pltpu.VMEM((GHOSTP, ROWS), F32),
            pltpu.VMEM((plane, GHOSTP, ROWS), BF),
            pltpu.VMEM((plane, GHOSTP, ROWS), BF),
            pltpu.VMEM((plane * GHOSTP, ROWS), F32),
            pltpu.VMEM((GROUP + GHOSTS, MODES, ROWS), BF),
            pltpu.VMEM((TILE_DEV, SLOTS, MODES, ROWS), BF),
            pltpu.VMEM((TILE_DEV, SLOTS, MODES, ROWS), BF),
            pltpu.VMEM((2 * SLOTS * TP, 128), F32),
            pltpu.VMEM((OUT_ROWS, SLOTS * TP), BF),
            pltpu.VMEM((8, 128), jnp.int32),
            pltpu.VMEM((NZ, 8, 128), jnp.int32),
            pltpu.VMEM((NX * NC, NZ, 8, 128), jnp.int32),
            pltpu.VMEM((128, GROUPS * 8), BF),
            pltpu.VMEM((GROUPS, 8, 128), BF),
            pltpu.VMEM((GROUPS, 8, 128), BF),
            pltpu.VMEM((MODES * MODES, MODES * MODES), BF),
            pltpu.VMEM((MODES * MODES, MODES * MODES), BF),
            pltpu.VMEM((NY, GROUP, MODES * MODES), BF),
            pltpu.VMEM((TILE_DEV, 1, ROWS), F32),
            dma((TILE_DEV,)),
            dma((3,)), dma((3, NQ)),
            one, one,
            dma((3,)),
            one, one,
            one, dma((2, NZ // 2 - 1, NQ)),
            one, dma((2, NZ // 2 + 1, NQ)),
            one, one,
            one, one, one, one,
            one, one,
            one, one,
            one,
        ],
        compiler_params=pltpu.CompilerParams(
            collective_id=0, has_side_effects=True, vmem_limit_bytes=56 * 2**20
        ),
    )(modes, fetch_list, fetch_list, cols, cols, a_tiles)
    return pl.pallas_call(
        settle,
        out_shape=shapes,
        in_specs=[hbm, hbm],
        out_specs=(hbm, hbm),
        scratch_shapes=[
            pltpu.VMEM((TILE_DEV, SLOTS, MODES, ROWS), BF),
            pltpu.VMEM((GROUP, MODES * MODES), F32),
            dma((PARTS + 1,)),
            dma((PARTS + 1,)),
        ],
    )(prolong, coarse)


def solution(mesh):
    in_specs = (
        P(("sub", "blk"), None, None, None),
        P(("sub", "blk"), None, None),
        P(("sub", "blk"), None),
        P(("sub", "blk"), None),
    )
    out_specs = (P(("sub", "blk"), None, None, None), P("sub", None))
    return jax.shard_map(shards, mesh=mesh, in_specs=in_specs, out_specs=out_specs, check_vma=False)
```

```python
import functools

import jax
import jax.numpy as jnp
from jax import lax
from jax.experimental import pallas as pl
from jax.experimental.pallas import tpu as pltpu
from jax.sharding import PartitionSpec as P

MESH = pl.DeviceIdType.MESH
BF = jnp.bfloat16
F32 = jnp.float32
NZ, NX, NC, NY = 8, 4, 2, 4
TILE_DEV = 24
SLOTS = 12
SLOTP = 16
TP = 32
ROWS = 128
MODES = 16
GROUP = 96
GROUPS = NZ * NX * NC
TILES = GROUP * GROUPS
PER_PEER = 5
GHOSTS = 130
GHOSTP = 144
LIST = 256
PARTS = 4
TOGETHER = 6
NQ = 4
PLANE = NX * NY
PQ = PLANE // NQ
OUT_ROWS = GROUP + GROUPS * 8
DAMPING = 2.0 / 3.0


def dev(z, x, c, y):
    return ((z * NX + x) * NC + c, y)


def rcopy(src, dst, send, recv, device):
    return pltpu.make_async_remote_copy(
        src_ref=src, dst_ref=dst, send_sem=send, recv_sem=recv, device_id=device, device_id_type=MESH
    )


def dot_t(a, b):
    return lax.dot_general(a, b, (((1,), (1,)), ((), ())), preferred_element_type=F32)


def body(
    modes, fetch_in, fetch_s, col_s, col_v, a_hbm, prolong, coarse,
    fetch_v, col_f, a_v, mf, s1, blocks, rows_f, lists_v, lists_s, stage, msg, got, got_f, table,
    pv, qv, flat, seg, req, idx1, idx2, target, out, back, pack, unpack, ysum, scales,
    a_sem, scat_s, scat_r, list_s, list_r, own_sem, all_s, all_r, ring_s, ring_r, sib_s, sib_r,
    ex_s, ex_r, id1_s, id1_r, id2_s, id2_r, c1_s, c1_r, y_s, y_r, p_sem,
):
    s = lax.axis_index("sub")
    y = lax.axis_index("blk")
    z, x, c = s // (NX * NC), lax.rem(s // NC, NX), lax.rem(s, NC)
    me = x * NY + y
    xc = x * NC + c
    right, left = dev(lax.rem(z + 1, NZ), x, c, y), dev(lax.rem(z + NZ - 1, NZ), x, c, y)
    sibling = dev(z, x, 1 - c, y)

    def plane(p, d=0):
        tx, ty = lax.rem(x + p // NY, NX), lax.rem(y + p % NY, NY)
        return tx * NY + ty, dev(lax.rem(z + d, NZ), tx, c, ty)

    def along_z(d):
        tz = lax.rem(z + d, NZ)
        return tz, dev(tz, x, c, y)

    def across(d):
        t = lax.rem(xc + d, NX * NC)
        return t, (z * NX * NC + t, y)

    def along_y(d):
        return dev(z, x, c, lax.rem(y + d, NY))

    barrier = pltpu.get_barrier_semaphore()
    partners = [plane(p, d)[1] for d in (0, 1, NZ - 1) for p in range(PLANE) if p or d]
    partners += [along_z(d)[1] for d in range(2, NZ - 1)]
    partners += [dev(z, lax.rem(x + d, NX), 1 - c, y) for d in range(NX)]
    for partner in partners:
        pl.semaphore_signal(barrier, inc=1, device_id=partner, device_id_type=MESH)

    mf[...] = modes[...].astype(F32).reshape(TILE_DEV * MODES, ROWS)
    for m in range(MODES):
        s1[m] = mf[pl.ds(m, TILE_DEV, stride=MODES), :].astype(BF)

    pl.semaphore_wait(barrier, len(partners))

    pltpu.make_async_copy(s1.at[me], blocks.at[z, c, me], scat_r.at[0, me // PQ]).start()
    for i in range(PLANE):
        for j, d in ((1, 1), (2, NZ - 1), (0, 0)):
            if i or d:
                t, device = plane(i * 7 % PLANE, d)
                rcopy(s1.at[t], blocks.at[z, c, me], scat_s.at[j], scat_r.at[j, me // PQ], device).start()

    def piece(k, core, q):
        return blocks.at[k, core, pl.ds(q * PQ, PQ)]

    def ring(way, step, q, k):
        part = piece(k, c, q)
        device = right if way == 0 else left
        rcopy(part, part, ring_s.at[0], ring_r.at[way, step - 1, q], device).start()

    def pass_on(way, step, q, k):
        part = piece(k, c, q)
        rcopy(part, part, sib_s.at[0], sib_r.at[way, step, q], sibling).start()

    def widen(k, core, q):
        for u in range(q * PQ, (q + 1) * PQ):
            base = ((k * NX + u // NY) * NC + core) * GROUP + u % NY * TILE_DEV
            rows_f[pl.ds(pl.multiple_of(base, 8), TILE_DEV), :] = blocks[k, core, u].astype(F32)

    def from_sibling(way, step, q, k):
        part = piece(k, 1 - c, q)
        rcopy(part, part, sib_s.at[0], sib_r.at[way, step, q], sibling).wait_recv()
        widen(k, 1 - c, q)

    last = NZ // 2

    def arrived(j, q, k):
        part = piece(k, c, q)
        rcopy(part, part, scat_s.at[0], scat_r.at[j, q], sibling).wait_recv()

    for q in range(NQ):
        for way in range(2):
            k = lax.rem(z + (NZ - 1, 1)[way], NZ)
            arrived(1 + way, q, k)
            ring(way, 1, q, k)
            pass_on(way, 1, q, k)
    for q in range(NQ):
        arrived(0, q, z)
        pass_on(0, 0, q, z)

    for t in range(TILE_DEV):
        pltpu.make_async_copy(a_hbm.at[t], a_v.at[t], a_sem.at[t]).start()

    lane = lax.broadcasted_iota(jnp.int32, (8, 128), 1)
    sub8 = lax.broadcasted_iota(jnp.int32, (8, 128), 0)
    request = jnp.full((8, 128), -1, jnp.int32)
    slots = col_v[...]
    colvec = slots
    fetch_v[...] = jnp.zeros((1, LIST), jnp.int32)
    fetch_v[:, :GHOSTS] = fetch_in[...]
    for h in range(GHOSTS):
        tile = fetch_s[0, h]
        group = tile // GROUP
        request = jnp.where(
            (lane == group) & (sub8 == h % PER_PEER), tile - group * GROUP, request
        )
        slots = jnp.where(colvec == GROUP + h, GROUP + group * 8 + h % PER_PEER, slots)
    req[...] = request
    col_f[...] = jnp.full((SLOTP, 128), -1, jnp.int32)
    col_f[:SLOTS, :TILE_DEV] = slots
    lane1 = lax.broadcasted_iota(jnp.int32, (1, 128), 1)
    rows = []
    for k0 in range(0, SLOTS, 4):
        row = col_f[k0 : k0 + 1, :]
        for j in range(1, 4):
            row = jnp.where(lane1 // TP == j, pltpu.roll(col_f[k0 + j : k0 + j + 1, :], TP * j, 1), row)
        rows.append(row)
    slots = jnp.concatenate(rows, axis=1)
    flat[...] = jnp.zeros((2 * SLOTS * TP + 4 * TP, 128), F32)

    pltpu.make_async_copy(fetch_v, lists_v.at[me], own_sem.at[0]).start()
    for p in range(1, NX * NY):
        rcopy(fetch_v, lists_v.at[me], list_s.at[0], list_r.at[0], plane(p)[1]).start()
    for d in range(1, NZ):
        rcopy(req, idx1.at[z], id1_s.at[0], id1_r.at[0], along_z(d)[1]).start()
    mine = table.at[pl.ds(y * TILE_DEV, TILE_DEV)]
    pltpu.make_async_copy(modes, mine, own_sem.at[1]).start()
    for d in range(1, NY):
        rcopy(modes, mine, all_s.at[0], all_r.at[0], along_y(d)).start()
    idx1[z] = request

    for q in range(NQ):
        widen(z, c, q)

    def side_two():
        pltpu.make_async_copy(fetch_v, lists_v.at[me], own_sem.at[0]).wait()
        others = lists_v.at[pl.ds(0, NX * NY - 1)]
        rcopy(others, others, list_s.at[0], list_r.at[0], sibling).wait_recv()
        pltpu.make_async_copy(lists_v, lists_s, own_sem.at[2]).start()
        others = idx1.at[pl.ds(0, NZ - 1)]
        rcopy(others, others, id1_s.at[0], id1_r.at[0], sibling).wait_recv()
        for d in range(1, NX * NC):
            rcopy(idx1, idx2.at[xc], id2_s.at[0], id2_r.at[0], across(d)[1]).start()
        idx2[xc] = idx1[...]

    events = []
    for step in range(2, last + 1):
        for q in range(NQ):
            for way in range(2):
                if step < last or q * 2 // NQ == way:
                    events.append((way, step, q))
    pending = [(0, 0, q, z) for q in range(NQ)]
    for q in range(NQ):
        for way in range(2):
            k = lax.rem(z + (NZ - 1, 1)[way], NZ)
            widen(k, c, q)
            pending.append((way, 1, q, k))
    for way, step, q in events:
        k = lax.rem(z + NZ - step, NZ) if way == 0 else lax.rem(z + step, NZ)
        part = piece(k, c, q)
        rcopy(part, part, ring_s.at[0], ring_r.at[way, step - 2, q], sibling).wait_recv()
        if step < last - 1 or (step == last - 1 and q * 2 // NQ == way):
            ring(way, step, q, k)
        pass_on(way, step, q, k)
        widen(k, c, q)
        pending.append((way, step, q, k))
        if (way, step, q) == (1, 2, NQ - 1):
            side_two()
        for _ in range(2):
            if len(pending) > 3:
                from_sibling(*pending.pop(0))
    pltpu.make_async_copy(lists_v, lists_s, own_sem.at[2]).wait()
    for item in pending:
        from_sibling(*item)

    def pick(t):
        for h in range(GHOSTS):
            stage[pl.ds(h, 1), :] = rows_f[pl.ds(lists_s[t, 0, h], 1), :]
        return stage[...].astype(BF)

    stage[pl.ds(GHOSTS - 2, GHOSTP - GHOSTS + 2), :] = jnp.zeros((GHOSTP - GHOSTS + 2, ROWS), F32)

    @pl.loop(1, NX * NY)
    def _(i):
        p = lax.rem(i * 7, NX * NY)
        tx, ty = lax.rem(x + p // NY, NX), lax.rem(y + lax.rem(p, NY), NY)
        t = tx * NY + ty
        msg[t] = pick(t)
        rcopy(msg.at[t], got.at[me], ex_s.at[0], ex_r.at[0], dev(z, tx, c, ty)).start()

    got[me] = pick(me)

    place = lax.broadcasted_iota(jnp.int32, (OUT_ROWS, SLOTS * TP), 0)
    seg[...] = (place == slots).astype(F32).astype(BF)
    others = idx2.at[pl.ds(0, NX * NC - 1)]
    rcopy(others, others, id2_s.at[0], id2_r.at[0], sibling).wait_recv()
    wanted = jnp.concatenate([idx2[g % (NX * NC), g // (NX * NC)] for g in range(GROUPS)], axis=0)
    lanes = lax.broadcasted_iota(jnp.int32, (GROUPS * 8, 128), 1)
    chosen = jnp.sum(jnp.where(lanes == s, wanted, 0).astype(F32), axis=1, keepdims=True)
    target[...] = (lanes.astype(F32) == chosen).astype(F32).T.astype(BF)

    full = MODES * MODES

    def pair(entry):
        m, n = entry // MODES, lax.rem(entry, MODES)
        high, low = jnp.maximum(m, n), jnp.minimum(m, n)
        return high * (high + 1) // 2 + low, m >= n

    def lane_pair(at):
        return jnp.where(at < 128, at, 128 + lax.rem(at, 8))

    down = lax.broadcasted_iota(jnp.int32, (full, full), 0)
    over = lax.broadcasted_iota(jnp.int32, (full, full), 1)
    index, kept = pair(down)
    pack[...] = ((index == lane_pair(over)) & kept).astype(F32).astype(BF)
    unpack[...] = (pair(over)[0] == lane_pair(down)).astype(F32).astype(BF)

    eye = lax.broadcasted_iota(jnp.int32, (ROWS, ROWS), 0) == lax.broadcasted_iota(
        jnp.int32, (ROWS, ROWS), 1
    )

    @pl.loop(0, TILE_DEV, step=4)
    def _(t0):
        for t in range(4):
            pltpu.make_async_copy(a_hbm.at[t0 + t], a_v.at[t0 + t], a_sem.at[t0 + t]).wait()
        for t in range(4):
            diagonal = jnp.sum(jnp.where(eye, a_v[t0 + t, 0].astype(F32), 0.0), axis=0, keepdims=True)
            scales[t0 + t] = DAMPING / diagonal

    pltpu.make_async_copy(modes, mine, own_sem.at[1]).wait()
    others = table.at[pl.ds(0, (NY - 1) * TILE_DEV)]
    rcopy(others, others, all_s.at[0], all_r.at[0], sibling).wait_recv()
    others = got.at[pl.ds(0, NX * NY - 1)]
    rcopy(others, others, ex_s.at[0], ex_r.at[0], sibling).wait_recv()
    for m in range(MODES):
        got_f[pl.ds(m * GHOSTP, GHOSTP), :] = got[m].astype(F32)
    for h in range(GHOSTS):
        table[GROUP + h] = got_f[pl.ds(h, MODES, stride=GHOSTP), :].astype(BF)

    n = SLOTS * MODES
    same_slot = (
        lax.broadcasted_iota(jnp.int32, (n, n), 0) // MODES
        == lax.broadcasted_iota(jnp.int32, (n, n), 1) // MODES
    )
    spread = (
        lax.rem(lax.broadcasted_iota(jnp.int32, (n, MODES * MODES), 0), MODES)
        == lax.rem(lax.broadcasted_iota(jnp.int32, (n, MODES * MODES), 1), MODES)
    ).astype(F32).astype(BF)
    same_mode = (
        lax.rem(lax.broadcasted_iota(jnp.int32, (n, MODES * MODES), 0), MODES)
        == lax.broadcasted_iota(jnp.int32, (n, MODES * MODES), 1) // MODES
    )
    fold = (
        lax.broadcasted_iota(jnp.int32, (SLOTP, n), 0)
        == lax.broadcasted_iota(jnp.int32, (SLOTP, n), 1) // MODES
    ).astype(F32).astype(BF)

    def products(t):
        scale = scales[t]
        for k in range(0, SLOTS, 2):
            columns = jnp.concatenate([table[col_s[k, t]], table[col_s[k + 1, t]]], axis=0)
            two = dot_t(columns, a_v[t, pl.ds(k, 2)].reshape(2 * ROWS, ROWS))
            parts = [two[:MODES, :ROWS], two[MODES:, ROWS:]]
            for j, product in enumerate(parts):
                value = -scale * product
                if k + j == 0:
                    value = modes[t].astype(F32) + value
                pv[t, k + j] = value.astype(BF)
                qv[t, k + j] = product.astype(BF)

    def pairs(t):
        both = dot_t(pv[t].reshape(n, ROWS), qv[t].reshape(n, ROWS)) * (1.0 / ROWS)
        return jnp.where(same_slot, both, 0.0).astype(BF)

    def widened(both):
        wide = jnp.dot(both, spread, preferred_element_type=F32)
        return jnp.where(same_mode, wide, 0.0)

    def folded(t, wide):
        res = jnp.dot(fold, wide.astype(BF), preferred_element_type=F32)
        flat[pl.ds(t, SLOTS, stride=TP), :] = res[:SLOTS, :128]
        flat[pl.ds(SLOTS * TP + t, SLOTS, stride=TP), :] = res[:SLOTS, 128:]

    @pl.loop(0, TILE_DEV, step=TOGETHER)
    def _(t0):
        for u in range(TOGETHER):
            products(t0 + u)

        bs = [pairs(t0 + u) for u in range(TOGETHER)]
        ws = [widened(v) for v in bs]
        for u in range(TOGETHER):
            folded(t0 + u, ws[u])

    pltpu.make_async_copy(pv, prolong, p_sem.at[0]).start()

    terms = jnp.concatenate([flat[: SLOTS * TP, :], flat[SLOTS * TP : 2 * SLOTS * TP, :]], axis=1).astype(BF)
    remote = jnp.dot(seg[GROUP:, :], terms, preferred_element_type=F32)
    packed = jnp.dot(remote.astype(BF), pack[...], preferred_element_type=F32)
    slot_row = lax.broadcasted_iota(jnp.int32, (GROUPS, 8, 128), 1)
    own_lanes = lax.broadcasted_iota(jnp.int32, (GROUPS, 8, 128), 2) // 8 == slot_row
    rest = jnp.where(own_lanes, packed[:, 128:].reshape(GROUPS, 8, 128), 0.0)
    rest = jnp.broadcast_to(jnp.sum(rest, axis=1, keepdims=True), (GROUPS, 8, 128))
    out[...] = jnp.where(slot_row == PER_PEER, rest, packed[:, :128].reshape(GROUPS, 8, 128)).astype(BF)

    @pl.loop(1, GROUPS, unroll=7)
    def _(d):
        t = lax.rem(s + d * 37, GROUPS)
        rcopy(out.at[t], back.at[s], c1_s.at[0], c1_r.at[0], (t, y)).start()

    back[s] = out[s]
    local = jnp.dot(seg[:GROUP, :], terms, preferred_element_type=F32)
    others = back.at[pl.ds(0, GROUPS - 1)]
    rcopy(others, others, c1_s.at[0], c1_r.at[0], sibling).wait_recv()
    came = back[...]
    rest = jnp.broadcast_to(came[:, PER_PEER : PER_PEER + 1, :].astype(F32), (GROUPS, 8, 128))
    rest = jnp.where(own_lanes, rest, 0.0).astype(BF)
    both = jnp.concatenate([came.reshape(GROUPS * 8, 128), rest.reshape(GROUPS * 8, 128)], axis=1)
    found = jnp.dot(target[...], both, preferred_element_type=F32)
    upper = found.astype(BF)
    lower = (found - upper.astype(F32)).astype(BF)
    returned = jnp.dot(upper, unpack[...], preferred_element_type=F32)
    returned = returned + jnp.dot(lower, unpack[...], preferred_element_type=F32)
    ysum[y] = (local + returned[:GROUP]).astype(BF)
    for d in range(1, NY):
        rcopy(ysum.at[y], ysum.at[y], y_s.at[0], y_r.at[0], along_y(d)).start()
    others = ysum.at[pl.ds(0, NY - 1)]
    rcopy(others, others, y_s.at[0], y_r.at[0], sibling).wait_recv()
    total = ysum[0].astype(F32)
    for k in range(1, NY):
        total = total + ysum[k].astype(F32)
    coarse[...] = total

    def sent(region, sem):
        rcopy(region, region, sem, sem, sibling).wait_send()

    sent(s1.at[pl.ds(0, PLANE - 1)], scat_s.at[0])
    sent(s1, scat_s.at[1])
    sent(s1, scat_s.at[2])
    sent(lists_v.at[pl.ds(0, NX * NY - 1)], list_s.at[0])
    sent(idx1.at[pl.ds(0, NZ - 1)], id1_s.at[0])
    sent(idx2.at[pl.ds(0, NX * NC - 1)], id2_s.at[0])
    sent(table.at[pl.ds(0, (NY - 1) * TILE_DEV)], all_s.at[0])
    sent(blocks.at[pl.ds(0, NZ - 3), c], ring_s.at[0])
    sent(blocks.at[:, c], sib_s.at[0])
    sent(msg.at[pl.ds(0, NX * NY - 1)], ex_s.at[0])
    sent(back.at[pl.ds(0, GROUPS - 1)], c1_s.at[0])
    sent(ysum.at[pl.ds(0, NY - 1)], y_s.at[0])
    pltpu.make_async_copy(pv, prolong, p_sem.at[0]).wait()


def settle(prolong_in, coarse_in, prolong, coarse, held, held_c, in_s, out_s):
    def parts(i):
        if i == PARTS:
            return coarse_in, held_c, coarse
        span = pl.ds(i * (TILE_DEV // PARTS), TILE_DEV // PARTS)
        return prolong_in.at[span], held.at[span], prolong.at[span]

    for i in range(PARTS + 1):
        src, mid, _ = parts(i)
        pltpu.make_async_copy(src, mid, in_s.at[i]).start()
    for i in range(PARTS + 1):
        src, mid, dst = parts(i)
        pltpu.make_async_copy(src, mid, in_s.at[i]).wait()
        pltpu.make_async_copy(mid, dst, out_s.at[i]).start()
    for i in range(PARTS + 1):
        _, mid, dst = parts(i)
        pltpu.make_async_copy(mid, dst, out_s.at[i]).wait()


def shards(a_tiles, modes, col_tiles, fetch_list):
    cols = col_tiles.T
    dma = pltpu.SemaphoreType.DMA
    vmem = pl.BlockSpec(memory_space=pltpu.VMEM)
    smem = pl.BlockSpec(memory_space=pltpu.SMEM)
    hbm = pl.BlockSpec(memory_space=pl.ANY)
    plane = NX * NY
    one = dma((1,))
    shapes = (
        jax.ShapeDtypeStruct((TILE_DEV, SLOTS, MODES, ROWS), BF),
        jax.ShapeDtypeStruct((GROUP, MODES * MODES), F32),
    )
    prolong, coarse = pl.pallas_call(
        body,
        out_shape=shapes,
        in_specs=[vmem, vmem, smem, smem, vmem, hbm],
        out_specs=(hbm, vmem),
        scratch_shapes=[
            pltpu.VMEM((1, LIST), jnp.int32),
            pltpu.VMEM((SLOTP, 128), jnp.int32),
            pltpu.VMEM((TILE_DEV, SLOTS, ROWS, ROWS), BF),
            pltpu.VMEM((TILE_DEV * MODES, ROWS), F32),
            pltpu.VMEM((MODES, TILE_DEV, ROWS), BF),
            pltpu.VMEM((NZ, NC, PLANE, TILE_DEV, ROWS), BF),
            pltpu.VMEM((TILES + 8, ROWS), F32),
            pltpu.VMEM((plane, 1, LIST), jnp.int32),
            pltpu.SMEM((plane, 1, LIST), jnp.int32),
            pltpu.VMEM((GHOSTP, ROWS), F32),
            pltpu.VMEM((plane, GHOSTP, ROWS), BF),
            pltpu.VMEM((plane, GHOSTP, ROWS), BF),
            pltpu.VMEM((plane * GHOSTP, ROWS), F32),
            pltpu.VMEM((GROUP + GHOSTS, MODES, ROWS), BF),
            pltpu.VMEM((TILE_DEV, SLOTS, MODES, ROWS), BF),
            pltpu.VMEM((TILE_DEV, SLOTS, MODES, ROWS), BF),
            pltpu.VMEM((2 * SLOTS * TP + 4 * TP, 128), F32),
            pltpu.VMEM((OUT_ROWS, SLOTS * TP), BF),
            pltpu.VMEM((8, 128), jnp.int32),
            pltpu.VMEM((NZ, 8, 128), jnp.int32),
            pltpu.VMEM((NX * NC, NZ, 8, 128), jnp.int32),
            pltpu.VMEM((128, GROUPS * 8), BF),
            pltpu.VMEM((GROUPS, 8, 128), BF),
            pltpu.VMEM((GROUPS, 8, 128), BF),
            pltpu.VMEM((MODES * MODES, MODES * MODES), BF),
            pltpu.VMEM((MODES * MODES, MODES * MODES), BF),
            pltpu.VMEM((NY, GROUP, MODES * MODES), BF),
            pltpu.VMEM((TILE_DEV, 1, ROWS), F32),
            dma((TILE_DEV,)),
            dma((3,)), dma((3, NQ)),
            one, one,
            dma((3,)),
            one, one,
            one, dma((2, NZ // 2 - 1, NQ)),
            one, dma((2, NZ // 2 + 1, NQ)),
            one, one,
            one, one, one, one,
            one, one,
            one, one,
            one,
        ],
        compiler_params=pltpu.CompilerParams(
            collective_id=0, has_side_effects=True, vmem_limit_bytes=56 * 2**20
        ),
    )(modes, fetch_list, fetch_list, cols, cols, a_tiles)
    return pl.pallas_call(
        settle,
        out_shape=shapes,
        in_specs=[hbm, hbm],
        out_specs=(hbm, hbm),
        scratch_shapes=[
            pltpu.VMEM((TILE_DEV, SLOTS, MODES, ROWS), BF),
            pltpu.VMEM((GROUP, MODES * MODES), F32),
            dma((PARTS + 1,)),
            dma((PARTS + 1,)),
        ],
    )(prolong, coarse)


def solution(mesh):
    in_specs = (
        P(("sub", "blk"), None, None, None),
        P(("sub", "blk"), None, None),
        P(("sub", "blk"), None),
        P(("sub", "blk"), None),
    )
    out_specs = (P(("sub", "blk"), None, None, None), P("sub", None))
    return jax.shard_map(shards, mesh=mesh, in_specs=in_specs, out_specs=out_specs, check_vma=False)
```

```python
import functools

import jax
import jax.numpy as jnp
from jax import lax
from jax.experimental import pallas as pl
from jax.experimental.pallas import tpu as pltpu
from jax.sharding import PartitionSpec as P

MESH = pl.DeviceIdType.MESH
BF = jnp.bfloat16
F32 = jnp.float32
NZ, NX, NC, NY = 8, 4, 2, 4
TILE_DEV = 24
SLOTS = 12
SLOTP = 16
TP = 32
ROWS = 128
MODES = 16
GROUP = 96
GROUPS = NZ * NX * NC
TILES = GROUP * GROUPS
PER_PEER = 5
GHOSTS = 130
GHOSTP = 144
LIST = 256
PARTS = 4
TOGETHER = 8
NQ = 4
PLANE = NX * NY
PQ = PLANE // NQ
OUT_ROWS = GROUP + GROUPS * 8
DAMPING = 2.0 / 3.0


def dev(z, x, c, y):
    return ((z * NX + x) * NC + c, y)


def rcopy(src, dst, send, recv, device):
    return pltpu.make_async_remote_copy(
        src_ref=src, dst_ref=dst, send_sem=send, recv_sem=recv, device_id=device, device_id_type=MESH
    )


def dot_t(a, b):
    return lax.dot_general(a, b, (((1,), (1,)), ((), ())), preferred_element_type=F32)


def body(
    modes, fetch_in, fetch_s, col_s, col_v, a_hbm, prolong, coarse,
    fetch_v, col_f, a_v, mf, s1, blocks, rows_f, lists_v, lists_s, stage, msg, got, got_f, table,
    pv, qv, flat, seg, req, idx1, idx2, target, out, back, pack, unpack, ysum, scales,
    a_sem, scat_s, scat_r, list_s, list_r, own_sem, all_s, all_r, ring_s, ring_r, sib_s, sib_r,
    ex_s, ex_r, id1_s, id1_r, id2_s, id2_r, c1_s, c1_r, y_s, y_r, p_sem,
):
    s = lax.axis_index("sub")
    y = lax.axis_index("blk")
    z, x, c = s // (NX * NC), lax.rem(s // NC, NX), lax.rem(s, NC)
    me = x * NY + y
    xc = x * NC + c
    right, left = dev(lax.rem(z + 1, NZ), x, c, y), dev(lax.rem(z + NZ - 1, NZ), x, c, y)
    sibling = dev(z, x, 1 - c, y)

    def plane(p, d=0):
        tx, ty = lax.rem(x + p // NY, NX), lax.rem(y + p % NY, NY)
        return tx * NY + ty, dev(lax.rem(z + d, NZ), tx, c, ty)

    def along_z(d):
        tz = lax.rem(z + d, NZ)
        return tz, dev(tz, x, c, y)

    def across(d):
        t = lax.rem(xc + d, NX * NC)
        return t, (z * NX * NC + t, y)

    def along_y(d):
        return dev(z, x, c, lax.rem(y + d, NY))

    barrier = pltpu.get_barrier_semaphore()
    partners = [plane(p, d)[1] for d in (0, 1, NZ - 1) for p in range(PLANE) if p or d]
    partners += [along_z(d)[1] for d in range(2, NZ - 1)]
    partners.append(sibling)
    for partner in partners:
        pl.semaphore_signal(barrier, inc=1, device_id=partner, device_id_type=MESH)

    mf[...] = modes[...].astype(F32).reshape(TILE_DEV * MODES, ROWS)
    for m in range(MODES):
        s1[m] = mf[pl.ds(m, TILE_DEV, stride=MODES), :].astype(BF)

    pl.semaphore_wait(barrier, len(partners))

    pltpu.make_async_copy(s1.at[me], blocks.at[z, c, me], scat_r.at[0, me // PQ]).start()
    for i in range(PLANE):
        for j, d in ((1, 1), (2, NZ - 1), (0, 0)):
            if i or d:
                t, device = plane(i * 7 % PLANE, d)
                rcopy(s1.at[t], blocks.at[z, c, me], scat_s.at[j], scat_r.at[j, me // PQ], device).start()

    def piece(k, core, q):
        return blocks.at[k, core, pl.ds(q * PQ, PQ)]

    def ring(way, step, q, k):
        part = piece(k, c, q)
        device = right if way == 0 else left
        rcopy(part, part, ring_s.at[0], ring_r.at[way, step - 1, q], device).start()

    def pass_on(way, step, q, k):
        part = piece(k, c, q)
        rcopy(part, part, sib_s.at[0], sib_r.at[way, step, q], sibling).start()

    def widen(k, core, q):
        for u in range(q * PQ, (q + 1) * PQ):
            base = ((k * NX + u // NY) * NC + core) * GROUP + u % NY * TILE_DEV
            rows_f[pl.ds(pl.multiple_of(base, 8), TILE_DEV), :] = blocks[k, core, u].astype(F32)

    def from_sibling(way, step, q, k):
        part = piece(k, 1 - c, q)
        rcopy(part, part, sib_s.at[0], sib_r.at[way, step, q], sibling).wait_recv()
        widen(k, 1 - c, q)

    last = NZ // 2

    def arrived(j, q, k):
        part = piece(k, c, q)
        rcopy(part, part, scat_s.at[0], scat_r.at[j, q], sibling).wait_recv()

    for q in range(NQ):
        for way in range(2):
            k = lax.rem(z + (NZ - 1, 1)[way], NZ)
            arrived(1 + way, q, k)
            ring(way, 1, q, k)
            pass_on(way, 1, q, k)
    for q in range(NQ):
        arrived(0, q, z)
        pass_on(0, 0, q, z)

    for t in range(TILE_DEV):
        pltpu.make_async_copy(a_hbm.at[t], a_v.at[t], a_sem.at[t]).start()

    lane = lax.broadcasted_iota(jnp.int32, (8, 128), 1)
    sub8 = lax.broadcasted_iota(jnp.int32, (8, 128), 0)
    request = jnp.full((8, 128), -1, jnp.int32)
    slots = col_v[...]
    colvec = slots
    fetch_v[...] = jnp.zeros((1, LIST), jnp.int32)
    fetch_v[:, :GHOSTS] = fetch_in[...]
    for h in range(GHOSTS):
        tile = fetch_s[0, h]
        group = tile // GROUP
        request = jnp.where(
            (lane == group) & (sub8 == h % PER_PEER), tile - group * GROUP, request
        )
        slots = jnp.where(colvec == GROUP + h, GROUP + group * 8 + h % PER_PEER, slots)
    req[...] = request
    col_f[...] = jnp.full((SLOTP, 128), -1, jnp.int32)
    col_f[:SLOTS, :TILE_DEV] = slots
    lane1 = lax.broadcasted_iota(jnp.int32, (1, 128), 1)
    rows = []
    for k0 in range(0, SLOTS, 4):
        row = col_f[k0 : k0 + 1, :]
        for j in range(1, 4):
            row = jnp.where(lane1 // TP == j, pltpu.roll(col_f[k0 + j : k0 + j + 1, :], TP * j, 1), row)
        rows.append(row)
    slots = jnp.concatenate(rows, axis=1)
    flat[...] = jnp.zeros((2 * SLOTS * TP + 4 * TP, 128), F32)

    pltpu.make_async_copy(fetch_v, lists_v.at[me], own_sem.at[0]).start()
    for p in range(1, NX * NY):
        rcopy(fetch_v, lists_v.at[me], list_s.at[0], list_r.at[0], plane(p)[1]).start()
    for d in range(1, NZ):
        rcopy(req, idx1.at[z], id1_s.at[0], id1_r.at[0], along_z(d)[1]).start()
    mine = table.at[pl.ds(y * TILE_DEV, TILE_DEV)]
    pltpu.make_async_copy(modes, mine, own_sem.at[1]).start()
    for d in range(1, NY):
        rcopy(modes, mine, all_s.at[0], all_r.at[0], along_y(d)).start()
    idx1[z] = request

    for q in range(NQ):
        widen(z, c, q)

    def side_two():
        pltpu.make_async_copy(fetch_v, lists_v.at[me], own_sem.at[0]).wait()
        others = lists_v.at[pl.ds(0, NX * NY - 1)]
        rcopy(others, others, list_s.at[0], list_r.at[0], sibling).wait_recv()
        pltpu.make_async_copy(lists_v, lists_s, own_sem.at[2]).start()
        others = idx1.at[pl.ds(0, NZ - 1)]
        rcopy(others, others, id1_s.at[0], id1_r.at[0], sibling).wait_recv()
        for d in range(1, NX * NC):
            rcopy(idx1, idx2.at[xc], id2_s.at[0], id2_r.at[0], across(d)[1]).start()
        idx2[xc] = idx1[...]

    events = []
    for step in range(2, last + 1):
        for q in range(NQ):
            for way in range(2):
                if step < last or q * 2 // NQ == way:
                    events.append((way, step, q))
    pending = [(0, 0, q, z) for q in range(NQ)]
    for q in range(NQ):
        for way in range(2):
            k = lax.rem(z + (NZ - 1, 1)[way], NZ)
            widen(k, c, q)
            pending.append((way, 1, q, k))
    for way, step, q in events:
        k = lax.rem(z + NZ - step, NZ) if way == 0 else lax.rem(z + step, NZ)
        part = piece(k, c, q)
        rcopy(part, part, ring_s.at[0], ring_r.at[way, step - 2, q], sibling).wait_recv()
        if step < last - 1 or (step == last - 1 and q * 2 // NQ == way):
            ring(way, step, q, k)
        pass_on(way, step, q, k)
        widen(k, c, q)
        pending.append((way, step, q, k))
        if (way, step, q) == (1, 2, NQ - 1):
            side_two()
        for _ in range(2):
            if len(pending) > 3:
                from_sibling(*pending.pop(0))
    pltpu.make_async_copy(lists_v, lists_s, own_sem.at[2]).wait()
    for item in pending:
        from_sibling(*item)

    def pick(t):
        for h in range(GHOSTS):
            stage[pl.ds(h, 1), :] = rows_f[pl.ds(lists_s[t, 0, h], 1), :]
        return stage[...].astype(BF)

    stage[pl.ds(GHOSTS - 2, GHOSTP - GHOSTS + 2), :] = jnp.zeros((GHOSTP - GHOSTS + 2, ROWS), F32)

    @pl.loop(1, NX * NY)
    def _(i):
        p = lax.rem(i * 7, NX * NY)
        tx, ty = lax.rem(x + p // NY, NX), lax.rem(y + lax.rem(p, NY), NY)
        t = tx * NY + ty
        msg[t] = pick(t)
        rcopy(msg.at[t], got.at[me], ex_s.at[0], ex_r.at[0], dev(z, tx, c, ty)).start()

    got[me] = pick(me)

    place = lax.broadcasted_iota(jnp.int32, (OUT_ROWS, SLOTS * TP), 0)
    seg[...] = (place == slots).astype(F32).astype(BF)
    others = idx2.at[pl.ds(0, NX * NC - 1)]
    rcopy(others, others, id2_s.at[0], id2_r.at[0], sibling).wait_recv()
    wanted = jnp.concatenate([idx2[g % (NX * NC), g // (NX * NC)] for g in range(GROUPS)], axis=0)
    lanes = lax.broadcasted_iota(jnp.int32, (GROUPS * 8, 128), 1)
    chosen = jnp.sum(jnp.where(lanes == s, wanted, 0).astype(F32), axis=1, keepdims=True)
    target[...] = (lanes.astype(F32) == chosen).astype(F32).T.astype(BF)

    full = MODES * MODES

    def pair(entry):
        m, n = entry // MODES, lax.rem(entry, MODES)
        high, low = jnp.maximum(m, n), jnp.minimum(m, n)
        return high * (high + 1) // 2 + low, m >= n

    def lane_pair(at):
        return jnp.where(at < 128, at, 128 + lax.rem(at, 8))

    down = lax.broadcasted_iota(jnp.int32, (full, full), 0)
    over = lax.broadcasted_iota(jnp.int32, (full, full), 1)
    index, kept = pair(down)
    pack[...] = ((index == lane_pair(over)) & kept).astype(F32).astype(BF)
    unpack[...] = (pair(over)[0] == lane_pair(down)).astype(F32).astype(BF)

    eye = lax.broadcasted_iota(jnp.int32, (ROWS, ROWS), 0) == lax.broadcasted_iota(
        jnp.int32, (ROWS, ROWS), 1
    )

    @pl.loop(0, TILE_DEV, step=4)
    def _(t0):
        for t in range(4):
            pltpu.make_async_copy(a_hbm.at[t0 + t], a_v.at[t0 + t], a_sem.at[t0 + t]).wait()
        for t in range(4):
            diagonal = jnp.sum(jnp.where(eye, a_v[t0 + t, 0].astype(F32), 0.0), axis=0, keepdims=True)
            scales[t0 + t] = DAMPING / diagonal

    pltpu.make_async_copy(modes, mine, own_sem.at[1]).wait()
    others = table.at[pl.ds(0, (NY - 1) * TILE_DEV)]
    rcopy(others, others, all_s.at[0], all_r.at[0], sibling).wait_recv()
    others = got.at[pl.ds(0, NX * NY - 1)]
    rcopy(others, others, ex_s.at[0], ex_r.at[0], sibling).wait_recv()
    for m in range(MODES):
        got_f[pl.ds(m * GHOSTP, GHOSTP), :] = got[m].astype(F32)
    for h in range(GHOSTS):
        table[GROUP + h] = got_f[pl.ds(h, MODES, stride=GHOSTP), :].astype(BF)

    n = SLOTS * MODES
    same_slot = (
        lax.broadcasted_iota(jnp.int32, (n, n), 0) // MODES
        == lax.broadcasted_iota(jnp.int32, (n, n), 1) // MODES
    )
    spread = (
        lax.rem(lax.broadcasted_iota(jnp.int32, (n, MODES * MODES), 0), MODES)
        == lax.rem(lax.broadcasted_iota(jnp.int32, (n, MODES * MODES), 1), MODES)
    ).astype(F32).astype(BF)
    same_mode = (
        lax.rem(lax.broadcasted_iota(jnp.int32, (n, MODES * MODES), 0), MODES)
        == lax.broadcasted_iota(jnp.int32, (n, MODES * MODES), 1) // MODES
    )
    fold = (
        lax.broadcasted_iota(jnp.int32, (SLOTP, n), 0)
        == lax.broadcasted_iota(jnp.int32, (SLOTP, n), 1) // MODES
    ).astype(F32).astype(BF)

    def products(t):
        scale = scales[t]
        for k in range(0, SLOTS, 2):
            columns = jnp.concatenate([table[col_s[k, t]], table[col_s[k + 1, t]]], axis=0)
            two = dot_t(columns, a_v[t, pl.ds(k, 2)].reshape(2 * ROWS, ROWS))
            parts = [two[:MODES, :ROWS], two[MODES:, ROWS:]]
            for j, product in enumerate(parts):
                value = -scale * product
                if k + j == 0:
                    value = modes[t].astype(F32) + value
                pv[t, k + j] = value.astype(BF)
                qv[t, k + j] = product.astype(BF)

    def pairs(t):
        both = dot_t(pv[t].reshape(n, ROWS), qv[t].reshape(n, ROWS)) * (1.0 / ROWS)
        return jnp.where(same_slot, both, 0.0).astype(BF)

    def widened(both):
        wide = jnp.dot(both, spread, preferred_element_type=F32)
        return jnp.where(same_mode, wide, 0.0)

    def folded(t, wide):
        res = jnp.dot(fold, wide.astype(BF), preferred_element_type=F32)
        flat[pl.ds(t, SLOTS, stride=TP), :] = res[:SLOTS, :128]
        flat[pl.ds(SLOTS * TP + t, SLOTS, stride=TP), :] = res[:SLOTS, 128:]

    @pl.loop(0, TILE_DEV, step=TOGETHER)
    def _(t0):
        for u in range(TOGETHER):
            products(t0 + u)

        bs = [pairs(t0 + u) for u in range(TOGETHER)]
        ws = [widened(v) for v in bs]
        for u in range(TOGETHER):
            folded(t0 + u, ws[u])

    pltpu.make_async_copy(pv, prolong, p_sem.at[0]).start()

    terms = jnp.concatenate([flat[: SLOTS * TP, :], flat[SLOTS * TP : 2 * SLOTS * TP, :]], axis=1).astype(BF)
    remote = jnp.dot(seg[GROUP:, :], terms, preferred_element_type=F32)
    packed = jnp.dot(remote.astype(BF), pack[...], preferred_element_type=F32)
    slot_row = lax.broadcasted_iota(jnp.int32, (GROUPS, 8, 128), 1)
    own_lanes = lax.broadcasted_iota(jnp.int32, (GROUPS, 8, 128), 2) // 8 == slot_row
    rest = jnp.where(own_lanes, packed[:, 128:].reshape(GROUPS, 8, 128), 0.0)
    rest = jnp.broadcast_to(jnp.sum(rest, axis=1, keepdims=True), (GROUPS, 8, 128))
    out[...] = jnp.where(slot_row == PER_PEER, rest, packed[:, :128].reshape(GROUPS, 8, 128)).astype(BF)

    @pl.loop(1, GROUPS, unroll=7)
    def _(d):
        t = lax.rem(s + d * 37, GROUPS)
        rcopy(out.at[t], back.at[s], c1_s.at[0], c1_r.at[0], (t, y)).start()

    back[s] = out[s]
    local = jnp.dot(seg[:GROUP, :], terms, preferred_element_type=F32)
    others = back.at[pl.ds(0, GROUPS - 1)]
    rcopy(others, others, c1_s.at[0], c1_r.at[0], sibling).wait_recv()
    came = back[...]
    rest = jnp.broadcast_to(came[:, PER_PEER : PER_PEER + 1, :].astype(F32), (GROUPS, 8, 128))
    rest = jnp.where(own_lanes, rest, 0.0).astype(BF)
    both = jnp.concatenate([came.reshape(GROUPS * 8, 128), rest.reshape(GROUPS * 8, 128)], axis=1)
    found = jnp.dot(target[...], both, preferred_element_type=F32)
    upper = found.astype(BF)
    lower = (found - upper.astype(F32)).astype(BF)
    returned = jnp.dot(upper, unpack[...], preferred_element_type=F32)
    returned = returned + jnp.dot(lower, unpack[...], preferred_element_type=F32)
    ysum[y] = (local + returned[:GROUP]).astype(BF)
    for d in range(1, NY):
        rcopy(ysum.at[y], ysum.at[y], y_s.at[0], y_r.at[0], along_y(d)).start()
    others = ysum.at[pl.ds(0, NY - 1)]
    rcopy(others, others, y_s.at[0], y_r.at[0], sibling).wait_recv()
    total = ysum[0].astype(F32)
    for k in range(1, NY):
        total = total + ysum[k].astype(F32)
    coarse[...] = total

    def sent(region, sem):
        rcopy(region, region, sem, sem, sibling).wait_send()

    sent(s1.at[pl.ds(0, PLANE - 1)], scat_s.at[0])
    sent(s1, scat_s.at[1])
    sent(s1, scat_s.at[2])
    sent(lists_v.at[pl.ds(0, NX * NY - 1)], list_s.at[0])
    sent(idx1.at[pl.ds(0, NZ - 1)], id1_s.at[0])
    sent(idx2.at[pl.ds(0, NX * NC - 1)], id2_s.at[0])
    sent(table.at[pl.ds(0, (NY - 1) * TILE_DEV)], all_s.at[0])
    sent(blocks.at[pl.ds(0, NZ - 3), c], ring_s.at[0])
    sent(blocks.at[:, c], sib_s.at[0])
    sent(msg.at[pl.ds(0, NX * NY - 1)], ex_s.at[0])
    sent(back.at[pl.ds(0, GROUPS - 1)], c1_s.at[0])
    sent(ysum.at[pl.ds(0, NY - 1)], y_s.at[0])
    pltpu.make_async_copy(pv, prolong, p_sem.at[0]).wait()


def settle(prolong_in, coarse_in, prolong, coarse, held, held_c, in_s, out_s):
    def parts(i):
        if i == PARTS:
            return coarse_in, held_c, coarse
        span = pl.ds(i * (TILE_DEV // PARTS), TILE_DEV // PARTS)
        return prolong_in.at[span], held.at[span], prolong.at[span]

    for i in range(PARTS + 1):
        src, mid, _ = parts(i)
        pltpu.make_async_copy(src, mid, in_s.at[i]).start()
    for i in range(PARTS + 1):
        src, mid, dst = parts(i)
        pltpu.make_async_copy(src, mid, in_s.at[i]).wait()
        pltpu.make_async_copy(mid, dst, out_s.at[i]).start()
    for i in range(PARTS + 1):
        _, mid, dst = parts(i)
        pltpu.make_async_copy(mid, dst, out_s.at[i]).wait()


def shards(a_tiles, modes, col_tiles, fetch_list):
    cols = col_tiles.T
    dma = pltpu.SemaphoreType.DMA
    vmem = pl.BlockSpec(memory_space=pltpu.VMEM)
    smem = pl.BlockSpec(memory_space=pltpu.SMEM)
    hbm = pl.BlockSpec(memory_space=pl.ANY)
    plane = NX * NY
    one = dma((1,))
    shapes = (
        jax.ShapeDtypeStruct((TILE_DEV, SLOTS, MODES, ROWS), BF),
        jax.ShapeDtypeStruct((GROUP, MODES * MODES), F32),
    )
    prolong, coarse = pl.pallas_call(
        body,
        out_shape=shapes,
        in_specs=[vmem, vmem, smem, smem, vmem, hbm],
        out_specs=(hbm, vmem),
        scratch_shapes=[
            pltpu.VMEM((1, LIST), jnp.int32),
            pltpu.VMEM((SLOTP, 128), jnp.int32),
            pltpu.VMEM((TILE_DEV, SLOTS, ROWS, ROWS), BF),
            pltpu.VMEM((TILE_DEV * MODES, ROWS), F32),
            pltpu.VMEM((MODES, TILE_DEV, ROWS), BF),
            pltpu.VMEM((NZ, NC, PLANE, TILE_DEV, ROWS), BF),
            pltpu.VMEM((TILES + 8, ROWS), F32),
            pltpu.VMEM((plane, 1, LIST), jnp.int32),
            pltpu.SMEM((plane, 1, LIST), jnp.int32),
            pltpu.VMEM((GHOSTP, ROWS), F32),
            pltpu.VMEM((plane, GHOSTP, ROWS), BF),
            pltpu.VMEM((plane, GHOSTP, ROWS), BF),
            pltpu.VMEM((plane * GHOSTP, ROWS), F32),
            pltpu.VMEM((GROUP + GHOSTS, MODES, ROWS), BF),
            pltpu.VMEM((TILE_DEV, SLOTS, MODES, ROWS), BF),
            pltpu.VMEM((TILE_DEV, SLOTS, MODES, ROWS), BF),
            pltpu.VMEM((2 * SLOTS * TP + 4 * TP, 128), F32),
            pltpu.VMEM((OUT_ROWS, SLOTS * TP), BF),
            pltpu.VMEM((8, 128), jnp.int32),
            pltpu.VMEM((NZ, 8, 128), jnp.int32),
            pltpu.VMEM((NX * NC, NZ, 8, 128), jnp.int32),
            pltpu.VMEM((128, GROUPS * 8), BF),
            pltpu.VMEM((GROUPS, 8, 128), BF),
            pltpu.VMEM((GROUPS, 8, 128), BF),
            pltpu.VMEM((MODES * MODES, MODES * MODES), BF),
            pltpu.VMEM((MODES * MODES, MODES * MODES), BF),
            pltpu.VMEM((NY, GROUP, MODES * MODES), BF),
            pltpu.VMEM((TILE_DEV, 1, ROWS), F32),
            dma((TILE_DEV,)),
            dma((3,)), dma((3, NQ)),
            one, one,
            dma((3,)),
            one, one,
            one, dma((2, NZ // 2 - 1, NQ)),
            one, dma((2, NZ // 2 + 1, NQ)),
            one, one,
            one, one, one, one,
            one, one,
            one, one,
            one,
        ],
        compiler_params=pltpu.CompilerParams(
            collective_id=0, has_side_effects=True, vmem_limit_bytes=56 * 2**20
        ),
    )(modes, fetch_list, fetch_list, cols, cols, a_tiles)
    return pl.pallas_call(
        settle,
        out_shape=shapes,
        in_specs=[hbm, hbm],
        out_specs=(hbm, hbm),
        scratch_shapes=[
            pltpu.VMEM((TILE_DEV, SLOTS, MODES, ROWS), BF),
            pltpu.VMEM((GROUP, MODES * MODES), F32),
            dma((PARTS + 1,)),
            dma((PARTS + 1,)),
        ],
    )(prolong, coarse)


def solution(mesh):
    in_specs = (
        P(("sub", "blk"), None, None, None),
        P(("sub", "blk"), None, None),
        P(("sub", "blk"), None),
        P(("sub", "blk"), None),
    )
    out_specs = (P(("sub", "blk"), None, None, None), P("sub", None))
    return jax.shard_map(shards, mesh=mesh, in_specs=in_specs, out_specs=out_specs, check_vma=False)
```
